512 devices in a mesh: row: 16 (over y, x_lo), col: 16 (over z, core), lag: 2 (over x_hi).
Axes of the slice: x: 4 (x_hi: 2, x_lo: 2; x = x_hi * 2 + x_lo), y: 8, z: 8, core: 2. Of those that a mesh axis runs over, the one named last changes fastest.
Arguments:
- trajectories: bfloat16 [16384, 4096], P(('row', 'col'), 'lag'), may hold values from -6 to 6
- pair_live: int32 [16, 16], replicated, may hold values from 0 to 1, as said below
Outputs:
- gram: bfloat16 [16384, 16384], P(('row', 'lag'), 'col')
The draws below stay inside these ranges and needn't reach their ends.
Inputs may be any that keep to these rules, and one draw needn't show every extreme that they name: `pair_live`: Symmetric, with every diagonal entry 1.
All inputs are finite; a program needn't handle non-finite values.
Results may differ from the reference program's by a relative error of at most 0.0015.
Values may be sent and summed in bfloat16 or wider, within the bound.
No kernel may reach another device: no remote copies, remote signals or barrier semaphores. Data moves between devices by JAX's collectives and lax.ppermute only.
A program may use at most 64 MiB of HBM per device.

```python
import math
import jax
import jax.numpy as jnp
from jax import lax

EMBED = 4096
TB = 1024
NB = 16
NT = 16384


def draw_trajectories(key, part):
    key_noise = jax.random.fold_in(key, 11)
    key_freq = jax.random.fold_in(key, 12)
    key_phase = jax.random.fold_in(key, 13)
    key_amp = jax.random.fold_in(key, 14)
    key_sigma = jax.random.fold_in(key, 15)
    noise = jnp.clip(jax.random.normal(key_noise, (NT, EMBED), jnp.float32), -4.0, 4.0)
    centre = 0.9
    spread = 0.75 * TB / EMBED
    freq = centre + spread * jax.random.uniform(key_freq, (NT,), jnp.float32, 0.0, 1.0)
    phase = jax.random.uniform(key_phase, (NT,), jnp.float32, -math.pi, math.pi)
    amp = jnp.exp(jax.random.uniform(key_amp, (NT,), jnp.float32, math.log(0.8), math.log(1.3)))
    sigma = jnp.exp(jax.random.uniform(key_sigma, (NT,), jnp.float32, math.log(0.3), math.log(0.6)))
    times = jnp.arange(EMBED, dtype=jnp.float32)
    wave = jnp.cos(freq[:, None] * times[None, :] + phase[:, None])
    values = amp[:, None] * wave + sigma[:, None] * noise
    return jnp.clip(values, -6.0, 6.0).astype(jnp.bfloat16)


def draw_pair_live(key, part):
    bits = jax.random.randint(jax.random.fold_in(key, 21), (NB, NB), 0, 2, jnp.int32)
    index = jnp.arange(NB, dtype=jnp.int32)
    upper = jnp.where(index[:, None] <= index[None, :], bits, bits.T)
    return jnp.where(index[:, None] == index[None, :], 1, upper).astype(jnp.int32)


def setup_inputs(seed: int = 0) -> dict:
    key_of = jax.random.split(jax.random.key(seed), 3)
    trajectories = draw_trajectories(jax.random.fold_in(key_of[2], 71), 0)
    pair_live = draw_pair_live(jax.random.fold_in(key_of[2], 71), 0)
    return {"trajectories": trajectories, "pair_live": pair_live}


def reference(trajectories, pair_live):
    floats = trajectories.astype(jnp.float32)
    norms = jnp.sum(floats * floats, axis=1)
    live_float = pair_live.astype(jnp.float32)

    def one_block(block_index):
        start = (block_index * TB).astype(jnp.int32)
        rows = lax.dynamic_slice_in_dim(trajectories, start, TB, 0)
        row_norm = lax.dynamic_slice_in_dim(norms, start, TB, 0)
        inner = jnp.dot(rows, trajectories.T, preferred_element_type=jnp.float32)
        dist = row_norm[:, None] + norms[None, :] - 2.0 * inner
        live_row = jnp.repeat(live_float[block_index], TB)
        return (jnp.exp(-2.0 * dist / EMBED) * live_row[None, :]).astype(jnp.bfloat16)

    blocks = lax.map(one_block, jnp.arange(NB, dtype=jnp.int32))
    return blocks.reshape(NT, NT)
```

```python
import jax
import jax.numpy as jnp
from jax import lax
from jax.experimental import pallas as pl
from jax.experimental.pallas import tpu as pltpu
from jax.sharding import Mesh
from jax.sharding import PartitionSpec as P

AX = ("y", "xl", "z", "a", "xh")
N = 8
SUB = 64


def every():
    for y in range(N):
        for xl in range(2):
            for z in range(N):
                for a in range(2):
                    for xh in range(2):
                        yield y, xl, z, a, xh


def index(y, xl, z, a, xh):
    return (((y % N * 2 + xl) * N + z % N) * 2 + a) * 2 + xh


def pairs(target):
    return [(index(*d), index(*target(*d))) for d in every()]


def row_pairs(stage):
    def target(y, xl, z, a, half):
        k = 2 * z + a
        return y, xl, k % N, k // N, half ^ xl ^ stage

    return pairs(target)


def col_pairs(stage):
    def target(y, xl, z, a, half):
        return y + (z if a == 0 else -z), half ^ xl ^ stage, y, a, xl

    return pairs(target)


def shift_y(step):
    return pairs(lambda y, xl, z, a, xh: (y + step, xl, z, a, xh))


def swap_core():
    return pairs(lambda y, xl, z, a, xh: (y, xl, z, 1 - a, xh))


def exchange():
    return pairs(
        lambda y, xl, z, a, xh: (y, xl, z, a, xh) if a == xh else (y, xl, z, xh, a)
    )


def gram_kernel(where_ref, rows_hbm, *refs):
    own, mate = refs[0:5], refs[5:10]
    out_ref, rows, cols, row_norm, sem_rows, sem_cols = refs[10:]
    y, z, a, live = where_ref[0], where_ref[1], where_ref[2], where_ref[3]
    rows_copy = pltpu.make_async_copy(rows_hbm, rows, sem_rows)
    rows_copy.start()
    copies = []
    for side, group in enumerate((own, mate)):
        core = a if side == 0 else 1 - a
        for d in range(-3, 5):
            ref = group[abs(d)]
            start = SUB if d < 0 else 0
            there = y - d
            m = jnp.where(core == 0, there - z, z - there) & (N - 1)
            copy = pltpu.make_async_copy(
                ref.at[pl.ds(start, SUB), :],
                cols.at[m, pl.ds(pl.multiple_of(core * SUB, SUB), SUB), :],
                sem_cols.at[side * N + d + 3],
            )
            copy.start()
            copies.append(copy)
    rows_copy.wait()

    @pl.loop(0, rows.shape[0] // 32)
    def _(i):
        at = pl.ds(pl.multiple_of(i * 32, 32), 32)
        total = jnp.zeros((32, 128), jnp.float32)
        for c in range(rows.shape[1] // 128):
            x = rows[at, c * 128 : (c + 1) * 128].astype(jnp.float32)
            total += x * x
        row_norm[at, :] = jnp.broadcast_to(
            jnp.sum(total, axis=1, keepdims=True), (32, 128)
        )

    for copy in copies:
        copy.wait()
    scale = live.astype(jnp.float32)
    samples = rows.shape[1]

    @pl.loop(0, 4)
    def _(i):
        b = cols[pl.ds(i * 2, 2)].reshape(256, samples)
        inner = lax.dot_general(
            rows[...], b, (((1,), (1,)), ((), ())), preferred_element_type=jnp.float32
        )
        total = jnp.zeros((256, 128), jnp.float32)
        for c in range(samples // 128):
            x = b[:, c * 128 : (c + 1) * 128].astype(jnp.float32)
            total += x * x
        col_norm = jnp.sum(total.T, axis=0, keepdims=True)
        dist = row_norm[:, :1] + col_norm - 2.0 * inner
        gram = jnp.exp(dist * (-2.0 / samples)) * scale
        out_ref[:, pl.ds(pl.multiple_of(i * 256, 256), 256)] = gram.astype(jnp.bfloat16)


def gram_tile(where, rows, own, mate):
    samples = rows.shape[1]
    anywhere = pl.BlockSpec(memory_space=pl.ANY)
    return pl.pallas_call(
        gram_kernel,
        out_shape=jax.ShapeDtypeStruct((512, 1024), jnp.bfloat16),
        in_specs=[pl.BlockSpec(memory_space=pltpu.SMEM)] + [anywhere] * 11,
        out_specs=pl.BlockSpec(memory_space=pltpu.VMEM),
        scratch_shapes=[
            pltpu.VMEM((512, samples), jnp.bfloat16),
            pltpu.VMEM((N, 2 * SUB, samples), jnp.bfloat16),
            pltpu.VMEM((512, 128), jnp.float32),
            pltpu.SemaphoreType.DMA,
            pltpu.SemaphoreType.DMA((2 * N,)),
        ],
        compiler_params=pltpu.CompilerParams(vmem_limit_bytes=32 * 1024 * 1024),
        cost_estimate=pl.CostEstimate(
            flops=2 * 512 * 1024 * samples,
            bytes_accessed=13 * 1024 * 1024,
            transcendentals=512 * 1024,
        ),
    )(where, rows, *own, *mate)


def on_device(trajectories, pair_live):
    y, xl, z, a, xh = (lax.axis_index(name) for name in AX)
    live = pair_live[y * 2 + xl, z * 2 + xh]
    send = lambda value, to: lax.ppermute(value, AX, to)

    rows = jnp.concatenate([send(trajectories, row_pairs(s)) for s in range(2)], axis=1)
    rows = lax.all_gather(rows, "z", axis=0, tiled=True)
    cols = jnp.concatenate([send(trajectories, col_pairs(s)) for s in range(2)], axis=1)

    own = [cols]
    up = down = cols
    for step in range(4):
        if step == 3:
            up, down = up[: SUB // 2], down[SUB // 2 :]
        up, down = send(up, shift_y(1)), send(down, shift_y(-1))
        own.append(jnp.concatenate([up, down], axis=0))
    mate = [send(chunk, swap_core()) for chunk in own]

    where = jnp.stack([y, z, a, live]).astype(jnp.int32)
    return send(gram_tile(where, rows, own, mate), exchange())


def solution(mesh):
    fine = Mesh(mesh.devices.reshape(N, 2, N, 2, 2), AX)
    return jax.shard_map(
        on_device,
        mesh=fine,
        in_specs=(P(("y", "xl", "z", "a"), "xh"), P()),
        out_specs=P(("y", "xl", "xh"), ("z", "a")),
        check_vma=False,
    )
```

```python
import jax
import jax.numpy as jnp
from jax import lax
from jax.experimental import pallas as pl
from jax.experimental.pallas import tpu as pltpu
from jax.sharding import Mesh
from jax.sharding import PartitionSpec as P

AX = ("y", "xl", "z", "a", "xh")
N = 8
SUB = 64
HALF = N * SUB
SHIFT = ((0, 4), (1, -1), (2, -2), (3, -3))


def index(y, xl, z, a, xh):
    return (((y % N * 2 + xl) * N + z % N) * 2 + a) * 2 + xh


def pairs(target):
    every = [
        (y, xl, z, a, xh)
        for y in range(N)
        for xl in range(2)
        for z in range(N)
        for a in range(2)
        for xh in range(2)
    ]
    return [(index(*d), index(*target(*d))) for d in every]


def col_pairs(stage):
    def target(y, xl, z, a, half):
        part = z // 4
        return y + SHIFT[z % 4][a], half ^ part ^ stage, y, xl, part

    return pairs(target)


def shift_z(step):
    return pairs(lambda y, xl, z, a, xh: (y, xl, z + step, a, xh))


def swap_core():
    return pairs(lambda y, xl, z, a, xh: (y, xl, z, 1 - a, xh))


def swap_lag():
    return pairs(lambda y, xl, z, a, xh: (y, xl, z, a, 1 - xh))


def chunks(own, mate):
    for d in range(-3, 5):
        step, first = abs(d), SUB if d < 0 else 0
        yield own[step], first, d, 0
        if step == 0:
            yield mate[0], 0, d, 1
        elif step < 3:
            yield mate[0], SUB + (step - 1) * 2 * SUB + first, d, 1
        else:
            yield mate[step - 2], first, d, 1


def gram_kernel(where_ref, cols_hbm, *refs):
    own, mate = refs[0:5], refs[5:8]
    out_ref, rows, cols, row_norm, sem_rows, sem_cols = refs[8:]
    y, z, a, half, live = (where_ref[i] for i in range(5))
    col_copies = []
    for there in range(N):
        o = (there - z) & (N - 1)
        j = jnp.where(o < 4, 2 * o, (17 - 2 * o) & (N - 1))
        copy = pltpu.make_async_copy(
            cols_hbm.at[pl.ds(there * SUB, SUB), :],
            cols.at[pl.ds(pl.multiple_of(j * SUB, SUB), SUB), :],
            sem_cols.at[there],
        )
        copy.start()
        col_copies.append(copy)
    row_copies = []
    for n, (ref, first, d, other) in enumerate(chunks(own, mate)):
        there = (z - d) & (N - 1)
        core = a if other == 0 else 1 - a
        at = (2 * there + core) & (N - 1)
        copy = pltpu.make_async_copy(
            ref.at[pl.ds(first, SUB), :],
            rows.at[pl.ds(pl.multiple_of(at * SUB, SUB), SUB), :],
            sem_rows.at[n],
        )
        mine = there // 4 == half
        pl.when(mine)(copy.start)
        row_copies.append((mine, copy))
    for mine, copy in row_copies:
        pl.when(mine)(copy.wait)

    @pl.loop(0, HALF // 32)
    def _(i):
        at = pl.ds(pl.multiple_of(i * 32, 32), 32)
        total = jnp.zeros((32, 128), jnp.float32)
        for c in range(rows.shape[1] // 128):
            x = rows[at, c * 128 : (c + 1) * 128].astype(jnp.float32)
            total += x * x
        row_norm[at, :] = jnp.broadcast_to(
            jnp.sum(total, axis=1, keepdims=True), (32, 128)
        )

    for copy in col_copies:
        copy.wait()
    scale = live.astype(jnp.float32)
    samples = rows.shape[1]

    @pl.loop(0, HALF // 256)
    def _(i):
        at = pl.ds(pl.multiple_of(i * 256, 256), 256)
        b = cols[at, :]
        inner = lax.dot_general(
            rows[...], b, (((1,), (1,)), ((), ())), preferred_element_type=jnp.float32
        )
        total = jnp.zeros((256, 128), jnp.float32)
        for c in range(samples // 128):
            x = b[:, c * 128 : (c + 1) * 128].astype(jnp.float32)
            total += x * x
        col_norm = jnp.sum(total.T, axis=0, keepdims=True)
        dist = row_norm[:, :1] + col_norm - 2.0 * inner
        gram = jnp.exp(dist * (-2.0 / samples)) * scale
        out_ref[:, at] = gram.astype(jnp.bfloat16)


def gram_tile(where, cols, own, mate):
    samples = cols.shape[1]
    anywhere = pl.BlockSpec(memory_space=pl.ANY)
    return pl.pallas_call(
        gram_kernel,
        out_shape=jax.ShapeDtypeStruct((HALF, HALF), jnp.bfloat16),
        in_specs=[pl.BlockSpec(memory_space=pltpu.SMEM)] + [anywhere] * 9,
        out_specs=pl.BlockSpec(memory_space=pltpu.VMEM),
        scratch_shapes=[
            pltpu.VMEM((HALF, samples), jnp.bfloat16),
            pltpu.VMEM((HALF, samples), jnp.bfloat16),
            pltpu.VMEM((HALF, 128), jnp.float32),
            pltpu.SemaphoreType.DMA((2 * N,)),
            pltpu.SemaphoreType.DMA((N,)),
        ],
        compiler_params=pltpu.CompilerParams(vmem_limit_bytes=48 * 1024 * 1024),
        cost_estimate=pl.CostEstimate(
            flops=2 * HALF * HALF * samples,
            bytes_accessed=9 * 1024 * 1024,
            transcendentals=HALF * HALF,
        ),
    )(where, cols, *own, *mate)


def on_device(trajectories, pair_live):
    y, xl, z, a, xh = (lax.axis_index(name) for name in AX)
    live = pair_live[y * 2 + xl, z * 2 + a]

    def send(value, to):
        return lax.ppermute(value, AX, to)

    early = send(trajectories, col_pairs(0))
    late = send(trajectories, col_pairs(1))
    other = send(trajectories, swap_lag())
    early, late, other = lax.optimization_barrier((early, late, other))
    cols = lax.all_gather(
        jnp.concatenate([early, late], axis=1), "y", axis=0, tiled=True
    )
    rows = jnp.where(
        xl == 0,
        jnp.concatenate([trajectories, other], axis=1),
        jnp.concatenate([other, trajectories], axis=1),
    )

    own, steps = [rows], []
    up = down = rows
    for step in range(4):
        if step == 3:
            up, down = up[: SUB // 2], down[SUB // 2 :]
        up, down = send(up, shift_z(1)), send(down, shift_z(-1))
        own.append(jnp.concatenate([up, down], axis=0))
    mate = [send(jnp.concatenate(own[:3], axis=0), swap_core())]
    mate += [send(chunk, swap_core()) for chunk in own[3:]]

    def tile(half):
        where = jnp.stack([y, z, a, half, live]).astype(jnp.int32)
        return gram_tile(where, cols, own, mate)

    given = send(tile(1 - xh), swap_lag())
    kept = tile(xh)
    return jnp.where(
        xh == 0,
        jnp.concatenate([kept, given], axis=1),
        jnp.concatenate([given, kept], axis=1),
    )


def solution(mesh):
    fine = Mesh(mesh.devices.reshape(N, 2, N, 2, 2), AX)
    return jax.shard_map(
        on_device,
        mesh=fine,
        in_specs=(P(("y", "xl", "z", "a"), "xh"), P()),
        out_specs=P(("y", "xl", "xh"), ("z", "a")),
        check_vma=False,
    )
```

```python
import functools

import jax
import jax.numpy as jnp
from jax import lax
from jax.experimental import pallas as pl
from jax.experimental.pallas import tpu as pltpu
from jax.sharding import Mesh
from jax.sharding import PartitionSpec as P

AX = ("y", "xl", "z", "a", "xh")
N = 8
SUB = 64
HALF = N * SUB
SHIFT = ((0, 4), (1, -1), (2, -2), (3, -3))


def index(y, xl, z, a, xh):
    return (((y % N * 2 + xl) * N + z % N) * 2 + a) * 2 + xh


def pairs(target):
    every = [
        (y, xl, z, a, xh)
        for y in range(N)
        for xl in range(2)
        for z in range(N)
        for a in range(2)
        for xh in range(2)
    ]
    return [(index(*d), index(*target(*d))) for d in every]


def col_pairs(stage):
    def target(y, xl, z, a, half):
        part = z // 4
        return y + SHIFT[z % 4][a], half ^ part ^ stage, y, xl, part

    return pairs(target)


def shift_z(step):
    return pairs(lambda y, xl, z, a, xh: (y, xl, z + step, a, xh))


def swap_core():
    return pairs(lambda y, xl, z, a, xh: (y, xl, z, 1 - a, xh))


def swap_lag():
    return pairs(lambda y, xl, z, a, xh: (y, xl, z, a, 1 - xh))


def chunks(own, mate):
    for d in range(-3, 5):
        step, first = abs(d), SUB if d < 0 else 0
        yield own[step], first, d, 0
        if step == 0:
            yield mate[0], 0, d, 1
        elif step < 3:
            yield mate[0], SUB + (step - 1) * 2 * SUB + first, d, 1
        else:
            yield mate[step - 2], first, d, 1


def square_sums(ref, first):
    total = jnp.zeros((SUB, 128), jnp.float32)
    for c in range(ref.shape[1] // 128):
        x = ref[pl.ds(first, SUB), c * 128 : (c + 1) * 128].astype(jnp.float32)
        total += x * x
    return total


def gram_kernel(keep, live_ref, cols_hbm, *refs):
    own, mate = refs[0:5], refs[5:8]
    out_ref, rows, cols, row_norm, col_norm, sem_rows, sem_cols = refs[8:]
    y, xl, z, a, xh = (lax.axis_index(name) for name in AX)
    half = xh if keep else 1 - xh
    samples = rows.shape[1]
    col_copies = []
    for there in range(N):
        o = (there - z) & (N - 1)
        j = jnp.where(o < 4, 2 * o, (17 - 2 * o) & (N - 1))
        first = pl.multiple_of(j * SUB, SUB)
        copy = pltpu.make_async_copy(
            cols_hbm.at[pl.ds(there * SUB, SUB), :],
            cols.at[pl.ds(first, SUB), :],
            sem_cols.at[there],
        )
        copy.start()
        col_copies.append((first, copy))
    row_copies = []
    for n, (ref, start, d, other) in enumerate(chunks(own, mate)):
        there = (z - d) & (N - 1)
        core = a if other == 0 else 1 - a
        first = pl.multiple_of(((2 * there + core) & (N - 1)) * SUB, SUB)
        copy = pltpu.make_async_copy(
            ref.at[pl.ds(start, SUB), :],
            rows.at[pl.ds(first, SUB), :],
            sem_rows.at[n],
        )
        mine = there // 4 == half
        pl.when(mine)(copy.start)
        row_copies.append((mine, first, copy))

    for first, copy in col_copies:
        copy.wait()
        col_norm[pl.ds(first, SUB), :] = square_sums(cols, first)
    for mine, first, copy in row_copies:

        @pl.when(mine)
        def _(first=first, copy=copy):
            copy.wait()
            total = jnp.sum(square_sums(rows, first), axis=1, keepdims=True)
            row_norm[pl.ds(first, SUB), :] = jnp.broadcast_to(total, (SUB, 128))

    scale = live_ref[2 * y + xl, 2 * z + a].astype(jnp.float32)
    base = xh * HALF if keep else 0

    @pl.loop(0, HALF // 256)
    def _(i):
        at = pl.ds(pl.multiple_of(i * 256, 256), 256)
        inner = lax.dot_general(
            rows[...],
            cols[at, :],
            (((1,), (1,)), ((), ())),
            preferred_element_type=jnp.float32,
        )
        across = jnp.sum(col_norm[at, :].T, axis=0, keepdims=True)
        dist = row_norm[:, :1] + across - 2.0 * inner
        gram = jnp.exp(dist * (-2.0 / samples)) * scale
        to = pl.ds(pl.multiple_of(base + i * 256, 256), 256)
        out_ref[:, to] = gram.astype(jnp.bfloat16)


def gram_tile(keep, pair_live, cols, own, mate):
    samples = cols.shape[1]
    anywhere = pl.BlockSpec(memory_space=pl.ANY)
    width = 2 * HALF if keep else HALF
    return pl.pallas_call(
        functools.partial(gram_kernel, keep),
        out_shape=jax.ShapeDtypeStruct((HALF, width), jnp.bfloat16),
        in_specs=[pl.BlockSpec(memory_space=pltpu.SMEM)] + [anywhere] * 9,
        out_specs=pl.BlockSpec(memory_space=pltpu.VMEM),
        scratch_shapes=[
            pltpu.VMEM((HALF, samples), jnp.bfloat16),
            pltpu.VMEM((HALF, samples), jnp.bfloat16),
            pltpu.VMEM((HALF, 128), jnp.float32),
            pltpu.VMEM((HALF, 128), jnp.float32),
            pltpu.SemaphoreType.DMA((2 * N,)),
            pltpu.SemaphoreType.DMA((N,)),
        ],
        compiler_params=pltpu.CompilerParams(vmem_limit_bytes=56 * 1024 * 1024),
        cost_estimate=pl.CostEstimate(
            flops=2 * HALF * HALF * samples,
            bytes_accessed=9 * 1024 * 1024,
            transcendentals=HALF * HALF,
        ),
    )(pair_live, cols, *own, *mate)


def on_device(trajectories, pair_live):
    xl, xh = lax.axis_index("xl"), lax.axis_index("xh")

    def send(value, to):
        return lax.ppermute(value, AX, to)

    other = send(trajectories, swap_lag())
    early = send(trajectories, col_pairs(0))
    late = send(trajectories, col_pairs(1))
    rows = jnp.where(
        xl == 0,
        jnp.concatenate([trajectories, other], axis=1),
        jnp.concatenate([other, trajectories], axis=1),
    )
    early, late, rows = lax.optimization_barrier((early, late, rows))
    cols = lax.all_gather(
        jnp.concatenate([early, late], axis=1), "y", axis=0, tiled=True
    )

    own = [rows]
    up = down = rows
    for step in range(4):
        if step == 3:
            up, down = up[: SUB // 2], down[SUB // 2 :]
        up, down = send(up, shift_z(1)), send(down, shift_z(-1))
        own.append(jnp.concatenate([up, down], axis=0))
    mate = [send(jnp.concatenate(own[:3], axis=0), swap_core())]
    mate += [send(chunk, swap_core()) for chunk in own[3:]]

    given = send(gram_tile(False, pair_live, cols, own, mate), swap_lag())
    kept = gram_tile(True, pair_live, cols, own, mate)
    return lax.dynamic_update_slice(kept, given, (0, (1 - xh) * HALF))


def solution(mesh):
    fine = Mesh(mesh.devices.reshape(N, 2, N, 2, 2), AX)
    return jax.shard_map(
        on_device,
        mesh=fine,
        in_specs=(P(("y", "xl", "z", "a"), "xh"), P()),
        out_specs=P(("y", "xl", "xh"), ("z", "a")),
        check_vma=False,
    )
```

```python
import functools

import jax
import jax.numpy as jnp
from jax import lax
from jax.experimental import pallas as pl
from jax.experimental.pallas import tpu as pltpu
from jax.sharding import Mesh
from jax.sharding import PartitionSpec as P

AX = ("y", "xl", "z", "a", "xh")
N = 8
SUB = 64
HALF = N * SUB
DEPTH = 1024
SHIFT = ((0, 4), (1, -1), (2, -2), (3, -3))
MIB = 1024 * 1024


def index(y, xl, z, a, xh):
    return (((y % N * 2 + xl) * N + z % N) * 2 + a) * 2 + xh


def pairs(target):
    every = [
        (y, xl, z, a, xh)
        for y in range(N)
        for xl in range(2)
        for z in range(N)
        for a in range(2)
        for xh in range(2)
    ]
    return [(index(*d), index(*target(*d))) for d in every]


def col_pairs(stage):
    def target(y, xl, z, a, half):
        part = z // 4
        return y + SHIFT[z % 4][a], half ^ part ^ stage, y, xl, part

    return pairs(target)


def shift_y(step):
    return pairs(lambda y, xl, z, a, xh: (y + step, xl, z, a, xh))


def swap_lag():
    return pairs(lambda y, xl, z, a, xh: (y, xl, z, a, 1 - xh))


def square_sums(x):
    total = jnp.zeros((x.shape[0], 128), jnp.float32)
    for c in range(x.shape[1] // 128):
        part = x[:, c * 128 : (c + 1) * 128].astype(jnp.float32)
        total += part * part
    return total


def place(d):
    o = (lax.axis_index("y") - d - lax.axis_index("z")) & (N - 1)
    j = jnp.where(o < 4, 2 * o, (17 - 2 * o) & (N - 1))
    return pl.multiple_of(j * SUB, SUB)


def order_kernel(chunks, *refs):
    count = len(chunks)
    sources = refs[:count]
    cols, norm, held, sums, sem = refs[-5:]
    copies = []
    for i, (source, (d, first, size)) in enumerate(zip(sources, chunks)):
        at = pl.ds(i * SUB, size)
        load = pltpu.make_async_copy(source, held.at[at, :], sem.at[0, i])
        load.start()
        copies.append((load, at, pl.ds(place(d) + first, size)))
    stores = []
    for i, (load, at, to) in enumerate(copies):
        load.wait()
        stores.append(
            pltpu.make_async_copy(held.at[at, :], cols.at[to, :], sem.at[1, i])
        )
        stores[-1].start()
        sums[at, :] = square_sums(held[at, :])
        stores.append(
            pltpu.make_async_copy(sums.at[at, :], norm.at[to, :], sem.at[2, i])
        )
        stores[-1].start()
    for store in stores:
        store.wait()


def in_order(chunks, sources, held=()):
    samples = sources[0].shape[1]
    count = len(chunks)
    return pl.pallas_call(
        functools.partial(order_kernel, chunks),
        out_shape=(
            jax.ShapeDtypeStruct((HALF, samples), jnp.bfloat16),
            jax.ShapeDtypeStruct((HALF, 128), jnp.float32),
        ),
        in_specs=[pl.BlockSpec(memory_space=pl.ANY)] * (count + len(held)),
        out_specs=[pl.BlockSpec(memory_space=pl.ANY)] * 2,
        input_output_aliases={count + i: i for i in range(len(held))},
        scratch_shapes=[
            pltpu.VMEM((count * SUB, samples), jnp.bfloat16),
            pltpu.VMEM((count * SUB, 128), jnp.float32),
            pltpu.SemaphoreType.DMA((3, count)),
        ],
        compiler_params=pltpu.CompilerParams(vmem_limit_bytes=16 * MIB),
        cost_estimate=pl.CostEstimate(
            flops=2 * count * SUB * samples,
            bytes_accessed=count * MIB,
            transcendentals=0,
        ),
    )(*sources, *held)


def gram_kernel(keep, live_ref, rows_hbm, cols_hbm, col_norm, out_ref, *scratch):
    rows, cols, inner, row_norm, sem = scratch
    y, xl, z, a, xh = (lax.axis_index(name) for name in AX)
    half = xh if keep else 1 - xh
    first = pl.multiple_of(half * HALF, HALF)
    blocks = rows.shape[0]
    samples = blocks * DEPTH
    copies = []
    for k in range(blocks):
        deep = pl.ds(k * DEPTH, DEPTH)
        copies.append(
            (
                pltpu.make_async_copy(cols_hbm.at[:, deep], cols.at[k], sem.at[0, k]),
                pltpu.make_async_copy(
                    rows_hbm.at[pl.ds(first, HALF), deep], rows.at[k], sem.at[1, k]
                ),
            )
        )
        for copy in copies[-1]:
            copy.start()
    for k in range(blocks):
        for copy in copies[k]:
            copy.wait()
        part = lax.dot_general(
            rows[k], cols[k], (((1,), (1,)), ((), ())), preferred_element_type=jnp.float32
        )
        norm = square_sums(rows[k])
        if k == 0:
            inner[...] = part
            row_norm[...] = norm
        else:
            inner[...] += part
            row_norm[...] += norm
    scale = live_ref[2 * y + xl, 2 * z + a].astype(jnp.float32)
    down = jnp.sum(row_norm[...], axis=1, keepdims=True)
    across = jnp.sum(col_norm[...].T, axis=0, keepdims=True)
    dist = down + across - 2.0 * inner[...]
    gram = jnp.exp(dist * (-2.0 / samples)) * scale
    base = pl.multiple_of(xh * HALF, HALF) if keep else 0
    out_ref[:, pl.ds(base, HALF)] = gram.astype(jnp.bfloat16)


def gram_tile(keep, pair_live, rows, cols, col_norm):
    samples = cols.shape[1]
    width = 2 * HALF if keep else HALF
    operand = pltpu.VMEM((samples // DEPTH, HALF, DEPTH), jnp.bfloat16)
    return pl.pallas_call(
        functools.partial(gram_kernel, keep),
        out_shape=jax.ShapeDtypeStruct((HALF, width), jnp.bfloat16),
        in_specs=[
            pl.BlockSpec(memory_space=pltpu.SMEM),
            pl.BlockSpec(memory_space=pl.ANY),
            pl.BlockSpec(memory_space=pl.ANY),
            pl.BlockSpec(memory_space=pltpu.VMEM),
        ],
        out_specs=pl.BlockSpec(memory_space=pltpu.VMEM),
        scratch_shapes=[
            operand,
            operand,
            pltpu.VMEM((HALF, HALF), jnp.float32),
            pltpu.VMEM((HALF, 128), jnp.float32),
            pltpu.SemaphoreType.DMA((2, samples // DEPTH)),
        ],
        compiler_params=pltpu.CompilerParams(vmem_limit_bytes=56 * MIB),
        cost_estimate=pl.CostEstimate(
            flops=2 * HALF * HALF * samples,
            bytes_accessed=9 * MIB,
            transcendentals=HALF * HALF,
        ),
    )(pair_live, rows, cols, col_norm)


def on_device(trajectories, pair_live):
    xl, xh = lax.axis_index("xl"), lax.axis_index("xh")

    def send(value, to):
        return lax.ppermute(value, AX, to)

    other = send(trajectories, swap_lag())
    early = send(trajectories, col_pairs(0))
    late = send(trajectories, col_pairs(1))
    rows = jnp.where(
        xl == 0,
        jnp.concatenate([trajectories, other], axis=1),
        jnp.concatenate([other, trajectories], axis=1),
    )
    rows = lax.all_gather(rows, ("z", "a"), axis=0, tiled=True)
    cols = jnp.concatenate([early, late], axis=1)

    chunks, sources = [(0, 0, SUB)], [cols]
    up = down = cols
    for step in range(1, N // 2):
        up, down = send(up, shift_y(1)), send(down, shift_y(-1))
        chunks += [(step, 0, SUB), (-step, 0, SUB)]
        sources += [up, down]
    most = in_order(chunks, sources)
    part = SUB // 2
    last = [send(up[:part], shift_y(1)), send(down[part:], shift_y(-1))]
    chunks = [(N // 2, 0, part), (N // 2, part, part)]
    cols, col_norm = in_order(chunks, last, most)

    given = send(gram_tile(False, pair_live, rows, cols, col_norm), swap_lag())
    kept = gram_tile(True, pair_live, rows, cols, col_norm)
    return lax.dynamic_update_slice(kept, given, (0, (1 - xh) * HALF))


def solution(mesh):
    fine = Mesh(mesh.devices.reshape(N, 2, N, 2, 2), AX)
    return jax.shard_map(
        on_device,
        mesh=fine,
        in_specs=(P(("y", "xl", "z", "a"), "xh"), P()),
        out_specs=P(("y", "xl", "xh"), ("z", "a")),
        check_vma=False,
    )
```

```python
import functools

import jax
import jax.numpy as jnp
from jax import lax
from jax.experimental import pallas as pl
from jax.experimental.pallas import tpu as pltpu
from jax.sharding import Mesh
from jax.sharding import PartitionSpec as P

AX = ("y", "xl", "z", "a", "xh")
N = 8
SUB = 64
HALF = N * SUB
DEPTH = 1024
SHIFT = ((0, 4), (1, -1), (2, -2), (3, -3))
MIB = 1024 * 1024


def index(y, xl, z, a, xh):
    return (((y % N * 2 + xl) * N + z % N) * 2 + a) * 2 + xh


def pairs(target):
    every = [
        (y, xl, z, a, xh)
        for y in range(N)
        for xl in range(2)
        for z in range(N)
        for a in range(2)
        for xh in range(2)
    ]
    return [(index(*d), index(*target(*d))) for d in every]


def col_half(z, xh):
    return xh ^ (z >> 1 & 1)


def col_pairs(stage):
    def target(y, xl, z, a, half):
        part = col_half(y, z // 4)
        return y + SHIFT[z % 4][a], half ^ part ^ stage, y, xl, part

    return pairs(target)


def shift_y(step):
    return pairs(lambda y, xl, z, a, xh: (y + step, xl, z, a, xh))


def swap_lag():
    return pairs(lambda y, xl, z, a, xh: (y, xl, z, a, 1 - xh))


def square_sums(x):
    total = jnp.zeros((x.shape[0], 128), jnp.float32)
    for c in range(x.shape[1] // 128):
        part = x[:, c * 128 : (c + 1) * 128].astype(jnp.float32)
        total += part * part
    return total


def place(d):
    o = (lax.axis_index("y") - d - lax.axis_index("z")) & (N - 1)
    j = jnp.where(o < 4, 2 * o, (17 - 2 * o) & (N - 1))
    return pl.multiple_of(j * SUB, SUB)


def order_kernel(chunks, *refs):
    count = len(chunks)
    sources = refs[:count]
    cols, norm, held, sums, sem = refs[-5:]
    copies = []
    for i, (source, (d, first, size)) in enumerate(zip(sources, chunks)):
        at = pl.ds(i * SUB, size)
        load = pltpu.make_async_copy(source, held.at[at, :], sem.at[0, i])
        load.start()
        copies.append((load, at, pl.ds(place(d) + first, size)))
    stores = []
    for i, (load, at, to) in enumerate(copies):
        load.wait()
        stores.append(
            pltpu.make_async_copy(held.at[at, :], cols.at[to, :], sem.at[1, i])
        )
        stores[-1].start()
        sums[at, :] = square_sums(held[at, :])
        stores.append(
            pltpu.make_async_copy(sums.at[at, :], norm.at[to, :], sem.at[2, i])
        )
        stores[-1].start()
    for store in stores:
        store.wait()


def in_order(chunks, sources, held=()):
    samples = sources[0].shape[1]
    count = len(chunks)
    return pl.pallas_call(
        functools.partial(order_kernel, chunks),
        out_shape=(
            jax.ShapeDtypeStruct((HALF, samples), jnp.bfloat16),
            jax.ShapeDtypeStruct((HALF, 128), jnp.float32),
        ),
        in_specs=[pl.BlockSpec(memory_space=pl.ANY)] * (count + len(held)),
        out_specs=[pl.BlockSpec(memory_space=pl.ANY)] * 2,
        input_output_aliases={count + i: i for i in range(len(held))},
        scratch_shapes=[
            pltpu.VMEM((count * SUB, samples), jnp.bfloat16),
            pltpu.VMEM((count * SUB, 128), jnp.float32),
            pltpu.SemaphoreType.DMA((3, count)),
        ],
        compiler_params=pltpu.CompilerParams(vmem_limit_bytes=56 * MIB),
        cost_estimate=pl.CostEstimate(
            flops=2 * count * SUB * samples,
            bytes_accessed=count * MIB,
            transcendentals=0,
        ),
    )(*sources, *held)


def gram_kernel(keep, live_ref, rows_hbm, cols_hbm, col_norm, out_ref, *scratch):
    rows, cols, inner, row_norm, sem = scratch
    y, xl, z, a, xh = (lax.axis_index(name) for name in AX)
    half = xh if keep else 1 - xh
    first = pl.multiple_of(half * HALF, HALF)
    blocks = rows.shape[0]
    samples = blocks * DEPTH
    copies = []
    for k in range(blocks):
        deep = pl.ds(k * DEPTH, DEPTH)
        copies.append(
            (
                pltpu.make_async_copy(cols_hbm.at[:, deep], cols.at[k], sem.at[0, k]),
                pltpu.make_async_copy(
                    rows_hbm.at[pl.ds(first, HALF), deep], rows.at[k], sem.at[1, k]
                ),
            )
        )
        for copy in copies[-1]:
            copy.start()
    for k in range(blocks):
        for copy in copies[k]:
            copy.wait()
        part = lax.dot_general(
            rows[k],
            cols[k],
            (((1,), (1,)), ((), ())),
            preferred_element_type=jnp.float32,
        )
        norm = square_sums(rows[k])
        if k == 0:
            inner[...] = part
            row_norm[...] = norm
        else:
            inner[...] += part
            row_norm[...] += norm
    scale = live_ref[2 * y + xl, 2 * z + a].astype(jnp.float32)
    down = jnp.sum(row_norm[...], axis=1, keepdims=True)
    across = jnp.sum(col_norm[...].T, axis=0, keepdims=True)
    dist = down + across - 2.0 * inner[...]
    gram = jnp.exp(dist * (-2.0 / samples)) * scale
    base = pl.multiple_of(col_half(z, xh) * HALF, HALF) if keep else 0
    out_ref[:, pl.ds(base, HALF)] = gram.astype(jnp.bfloat16)


def gram_tile(keep, pair_live, rows, cols, col_norm):
    samples = cols.shape[1]
    width = 2 * HALF if keep else HALF
    operand = pltpu.VMEM((samples // DEPTH, HALF, DEPTH), jnp.bfloat16)
    return pl.pallas_call(
        functools.partial(gram_kernel, keep),
        out_shape=jax.ShapeDtypeStruct((HALF, width), jnp.bfloat16),
        in_specs=[
            pl.BlockSpec(memory_space=pltpu.SMEM),
            pl.BlockSpec(memory_space=pl.ANY),
            pl.BlockSpec(memory_space=pl.ANY),
            pl.BlockSpec(memory_space=pltpu.VMEM),
        ],
        out_specs=pl.BlockSpec(memory_space=pltpu.VMEM),
        scratch_shapes=[
            operand,
            operand,
            pltpu.VMEM((HALF, HALF), jnp.float32),
            pltpu.VMEM((HALF, 128), jnp.float32),
            pltpu.SemaphoreType.DMA((2, samples // DEPTH)),
        ],
        compiler_params=pltpu.CompilerParams(vmem_limit_bytes=56 * MIB),
        cost_estimate=pl.CostEstimate(
            flops=2 * HALF * HALF * samples,
            bytes_accessed=9 * MIB,
            transcendentals=HALF * HALF,
        ),
    )(pair_live, rows, cols, col_norm)


def on_device(trajectories, pair_live):
    xl, z, xh = (lax.axis_index(name) for name in ("xl", "z", "xh"))

    def send(value, to):
        return lax.ppermute(value, AX, to)

    other = send(trajectories, swap_lag())
    early = send(trajectories, col_pairs(0))
    late = send(trajectories, col_pairs(1))
    early, late, other = lax.optimization_barrier((early, late, other))
    rows = jnp.where(
        xl == 0,
        jnp.concatenate([trajectories, other], axis=1),
        jnp.concatenate([other, trajectories], axis=1),
    )
    rows = lax.all_gather(rows, ("z", "a"), axis=0, tiled=True)
    cols = jnp.concatenate([early, late], axis=1)

    chunks, sources = [(0, 0, SUB)], [cols]
    up = down = cols
    for step in range(1, N // 2):
        up, down = send(up, shift_y(1)), send(down, shift_y(-1))
        chunks += [(step, 0, SUB), (-step, 0, SUB)]
        sources += [up, down]
    most = in_order(chunks, sources)
    part = SUB // 2
    last = [send(up[:part], shift_y(1)), send(down[part:], shift_y(-1))]
    chunks = [(N // 2, 0, part), (N // 2, part, part)]
    cols, col_norm = in_order(chunks, last, most)

    given = send(gram_tile(False, pair_live, rows, cols, col_norm), swap_lag())
    kept = gram_tile(True, pair_live, rows, cols, col_norm)
    return lax.dynamic_update_slice(kept, given, (0, (1 - col_half(z, xh)) * HALF))


def solution(mesh):
    fine = Mesh(mesh.devices.reshape(N, 2, N, 2, 2), AX)
    return jax.shard_map(
        on_device,
        mesh=fine,
        in_specs=(P(("y", "xl", "z", "a"), "xh"), P()),
        out_specs=P(("y", "xl", "xh"), ("z", "a")),
        check_vma=False,
    )
```

```python
import functools

import jax
import jax.numpy as jnp
from jax import lax
from jax.experimental import pallas as pl
from jax.experimental.pallas import tpu as pltpu
from jax.sharding import Mesh
from jax.sharding import PartitionSpec as P

AX = ("y", "xl", "z", "a", "xh")
N = 8
SUB = 64
HALF = N * SUB
DEPTH = 1024
SHIFT = ((0, 4), (1, -1), (2, -2), (3, -3))
MIB = 1024 * 1024


def index(y, xl, z, a, xh):
    return (((y % N * 2 + xl) * N + z % N) * 2 + a) * 2 + xh


def pairs(target):
    every = [
        (y, xl, z, a, xh)
        for y in range(N)
        for xl in range(2)
        for z in range(N)
        for a in range(2)
        for xh in range(2)
    ]
    return [(index(*d), index(*target(*d))) for d in every]


def col_half(z, xh):
    return xh ^ (z >> 1 & 1)


def col_pairs(stage):
    def target(y, xl, z, a, half):
        part = col_half(y, z // 4)
        return y + SHIFT[z % 4][a], half ^ part ^ stage, y, xl, part

    return pairs(target)


def shift_y(step):
    return pairs(lambda y, xl, z, a, xh: (y + step, xl, z, a, xh))


def swap_lag():
    return pairs(lambda y, xl, z, a, xh: (y, xl, z, a, 1 - xh))


def square_sums(x):
    total = jnp.zeros((x.shape[0], 128), jnp.float32)
    for c in range(x.shape[1] // 128):
        part = x[:, c * 128 : (c + 1) * 128].astype(jnp.float32)
        total += part * part
    return total


def place(d):
    o = (lax.axis_index("y") - d - lax.axis_index("z")) & (N - 1)
    j = jnp.where(o < 4, 2 * o, (17 - 2 * o) & (N - 1))
    return pl.multiple_of(j * SUB, SUB)


def order_kernel(steps, *refs):
    sources = refs[: 2 * len(steps)]
    cols, norm, held, sums, sem = refs[2 * len(steps) :]
    depth = held.shape[2]
    loads = [
        pltpu.make_async_copy(source, held.at[i], sem.at[0, i])
        for i, source in enumerate(sources)
    ]
    for load in loads:
        load.start()
    stores = []
    for n, d in enumerate(steps):
        to = pl.ds(place(d), SUB)
        for i in (2 * n, 2 * n + 1):
            loads[i].wait()
            deep = pl.ds((i % 2) * depth, depth)
            store = pltpu.make_async_copy(held.at[i], cols.at[to, deep], sem.at[1, i])
            store.start()
            stores.append(store)
        sums[n] = square_sums(held[2 * n]) + square_sums(held[2 * n + 1])
        store = pltpu.make_async_copy(sums.at[n], norm.at[to, :], sem.at[2, n])
        store.start()
        stores.append(store)
    for store in stores:
        store.wait()


def in_order(steps, sources):
    depth = sources[0].shape[1]
    count = len(sources)
    return pl.pallas_call(
        functools.partial(order_kernel, steps),
        out_shape=(
            jax.ShapeDtypeStruct((HALF, 2 * depth), jnp.bfloat16),
            jax.ShapeDtypeStruct((HALF, 128), jnp.float32),
        ),
        in_specs=[pl.BlockSpec(memory_space=pl.ANY)] * count,
        out_specs=[pl.BlockSpec(memory_space=pl.ANY)] * 2,
        scratch_shapes=[
            pltpu.VMEM((count, SUB, depth), jnp.bfloat16),
            pltpu.VMEM((len(steps), SUB, 128), jnp.float32),
            pltpu.SemaphoreType.DMA((3, count)),
        ],
        compiler_params=pltpu.CompilerParams(vmem_limit_bytes=56 * MIB),
        cost_estimate=pl.CostEstimate(
            flops=2 * count * SUB * depth,
            bytes_accessed=count * MIB // 2,
            transcendentals=0,
        ),
    )(*sources)


def gram_kernel(keep, live_ref, rows_hbm, cols_hbm, norm_ref, *refs):
    last, out_ref = refs[:2], refs[2]
    rows, cols, inner, row_norm, col_norm, sem = refs[3:]
    y, xl, z, a, xh = (lax.axis_index(name) for name in AX)
    half = xh if keep else 1 - xh
    first = pl.multiple_of(half * HALF, HALF)
    blocks = rows.shape[0]
    samples = blocks * DEPTH
    copies = []
    for k in range(blocks):
        deep = pl.ds(k * DEPTH, DEPTH)
        copies.append(
            (
                pltpu.make_async_copy(cols_hbm.at[:, deep], cols.at[k], sem.at[0, k]),
                pltpu.make_async_copy(
                    rows_hbm.at[pl.ds(first, HALF), deep], rows.at[k], sem.at[1, k]
                ),
            )
        )
        for copy in copies[-1]:
            copy.start()
    final = pl.ds(place(N // 2), SUB)
    col_norm[...] = norm_ref[...]
    col_norm[final, :] = square_sums(last[0]) + square_sums(last[1])
    for k in range(blocks):
        for copy in copies[k]:
            copy.wait()
        source, start = divmod(k * DEPTH, samples // 2)
        cols[k, final, :] = last[source][:, start : start + DEPTH]
        part = lax.dot_general(
            rows[k],
            cols[k],
            (((1,), (1,)), ((), ())),
            preferred_element_type=jnp.float32,
        )
        norm = square_sums(rows[k])
        if k == 0:
            inner[...] = part
            row_norm[...] = norm
        else:
            inner[...] += part
            row_norm[...] += norm
    scale = live_ref[2 * y + xl, 2 * z + a].astype(jnp.float32)
    down = jnp.sum(row_norm[...], axis=1, keepdims=True)
    across = jnp.sum(col_norm[...].T, axis=0, keepdims=True)
    dist = down + across - 2.0 * inner[...]
    gram = jnp.exp(dist * (-2.0 / samples)) * scale
    base = pl.multiple_of(col_half(z, xh) * HALF, HALF) if keep else 0
    out_ref[:, pl.ds(base, HALF)] = gram.astype(jnp.bfloat16)


def gram_tile(keep, pair_live, rows, cols, col_norm, last):
    samples = cols.shape[1]
    width = 2 * HALF if keep else HALF
    operand = pltpu.VMEM((samples // DEPTH, HALF, DEPTH), jnp.bfloat16)
    return pl.pallas_call(
        functools.partial(gram_kernel, keep),
        out_shape=jax.ShapeDtypeStruct((HALF, width), jnp.bfloat16),
        in_specs=[
            pl.BlockSpec(memory_space=pltpu.SMEM),
            pl.BlockSpec(memory_space=pl.ANY),
            pl.BlockSpec(memory_space=pl.ANY),
            pl.BlockSpec(memory_space=pltpu.VMEM),
            pl.BlockSpec(memory_space=pltpu.VMEM),
            pl.BlockSpec(memory_space=pltpu.VMEM),
        ],
        out_specs=pl.BlockSpec(memory_space=pltpu.VMEM),
        scratch_shapes=[
            operand,
            operand,
            pltpu.VMEM((HALF, HALF), jnp.float32),
            pltpu.VMEM((HALF, 128), jnp.float32),
            pltpu.VMEM((HALF, 128), jnp.float32),
            pltpu.SemaphoreType.DMA((2, samples // DEPTH)),
        ],
        compiler_params=pltpu.CompilerParams(vmem_limit_bytes=56 * MIB),
        cost_estimate=pl.CostEstimate(
            flops=2 * HALF * HALF * samples,
            bytes_accessed=9 * MIB,
            transcendentals=HALF * HALF,
        ),
    )(pair_live, rows, cols, col_norm, *last)


def on_device(trajectories, pair_live):
    xl, z, xh = (lax.axis_index(name) for name in ("xl", "z", "xh"))

    def send(value, to):
        return lax.ppermute(value, AX, to)

    other = send(trajectories, swap_lag())
    early = send(trajectories, col_pairs(0))
    late = send(trajectories, col_pairs(1))
    rows = jnp.where(
        xl == 0,
        jnp.concatenate([trajectories, other], axis=1),
        jnp.concatenate([other, trajectories], axis=1),
    )
    rows = lax.all_gather(rows, ("z", "a"), axis=0, tiled=True)

    steps, sources = [0], [early, late]
    up, down = [early, late], [early, late]
    for step in range(1, N // 2):
        up = [send(part, shift_y(1)) for part in up]
        down = [send(part, shift_y(-1)) for part in down]
        steps += [step, -step]
        sources += up + down
    cols, col_norm = in_order(steps, sources)
    last = [send(up[0], shift_y(1)), send(down[1], shift_y(-1))]

    given = send(gram_tile(False, pair_live, rows, cols, col_norm, last), swap_lag())
    kept = gram_tile(True, pair_live, rows, cols, col_norm, last)
    return lax.dynamic_update_slice(kept, given, (0, (1 - col_half(z, xh)) * HALF))


def solution(mesh):
    fine = Mesh(mesh.devices.reshape(N, 2, N, 2, 2), AX)
    return jax.shard_map(
        on_device,
        mesh=fine,
        in_specs=(P(("y", "xl", "z", "a"), "xh"), P()),
        out_specs=P(("y", "xl", "xh"), ("z", "a")),
        check_vma=False,
    )
```

```python
import functools

import jax
import jax.numpy as jnp
from jax import lax
from jax.experimental import pallas as pl
from jax.experimental.pallas import tpu as pltpu
from jax.sharding import Mesh
from jax.sharding import PartitionSpec as P

AX = ("y", "xl", "z", "a", "xh")
N = 8
SUB = 64
HALF = N * SUB
DEPTH = 1024
SHIFT = ((0, 4), (1, -1), (2, -2), (3, -3))
MIB = 1024 * 1024


def index(y, xl, z, a, xh):
    return (((y % N * 2 + xl) * N + z % N) * 2 + a) * 2 + xh


def pairs(target):
    every = [
        (y, xl, z, a, xh)
        for y in range(N)
        for xl in range(2)
        for z in range(N)
        for a in range(2)
        for xh in range(2)
    ]
    return [(index(*d), index(*target(*d))) for d in every]


def col_half(z, xh):
    return xh ^ (z >> 1 & 1)


def col_pairs(stage):
    def target(y, xl, z, a, half):
        part = col_half(y, z // 4)
        return y + SHIFT[z % 4][a], half ^ part ^ stage, y, xl, part

    return pairs(target)


def shift_y(step):
    return pairs(lambda y, xl, z, a, xh: (y + step, xl, z, a, xh))


def swap_lag():
    return pairs(lambda y, xl, z, a, xh: (y, xl, z, a, 1 - xh))


def square_sums(x):
    total = jnp.zeros((x.shape[0], 128), jnp.float32)
    for c in range(x.shape[1] // 128):
        part = x[:, c * 128 : (c + 1) * 128].astype(jnp.float32)
        total += part * part
    return total


def place(d):
    o = (lax.axis_index("y") - d - lax.axis_index("z")) & (N - 1)
    j = jnp.where(o < 4, 2 * o, (17 - 2 * o) & (N - 1))
    return pl.multiple_of(j * SUB, SUB)


def order_kernel(steps, *refs):
    sources = refs[: 2 * len(steps)]
    cols, norm, held, sums, sem = refs[2 * len(steps) :]
    depth = held.shape[2]
    loads = [
        pltpu.make_async_copy(source, held.at[i], sem.at[0, i])
        for i, source in enumerate(sources)
    ]
    for load in loads:
        load.start()
    stores = []
    for n, d in enumerate(steps):
        to = pl.ds(place(d), SUB)
        for i in (2 * n, 2 * n + 1):
            loads[i].wait()
            deep = pl.ds((i % 2) * depth, depth)
            store = pltpu.make_async_copy(held.at[i], cols.at[to, deep], sem.at[1, i])
            store.start()
            stores.append(store)
        sums[n] = square_sums(held[2 * n]) + square_sums(held[2 * n + 1])
        store = pltpu.make_async_copy(sums.at[n], norm.at[to, :], sem.at[2, n])
        store.start()
        stores.append(store)
    for store in stores:
        store.wait()


def in_order(steps, sources):
    depth = sources[0].shape[1]
    count = len(sources)
    return pl.pallas_call(
        functools.partial(order_kernel, steps),
        out_shape=(
            jax.ShapeDtypeStruct((HALF, 2 * depth), jnp.bfloat16),
            jax.ShapeDtypeStruct((HALF, 128), jnp.float32),
        ),
        in_specs=[pl.BlockSpec(memory_space=pl.ANY)] * count,
        out_specs=[pl.BlockSpec(memory_space=pl.ANY)] * 2,
        scratch_shapes=[
            pltpu.VMEM((count, SUB, depth), jnp.bfloat16),
            pltpu.VMEM((len(steps), SUB, 128), jnp.float32),
            pltpu.SemaphoreType.DMA((3, count)),
        ],
        compiler_params=pltpu.CompilerParams(vmem_limit_bytes=56 * MIB),
        cost_estimate=pl.CostEstimate(
            flops=2 * count * SUB * depth,
            bytes_accessed=count * MIB // 2,
            transcendentals=0,
        ),
    )(*sources)


def gram_kernel(keep, live_ref, rows_hbm, cols_hbm, norm_ref, *refs):
    last, out_ref = refs[:2], refs[2]
    rows, cols, inner, row_norm, col_norm, sem = refs[3:]
    y, xl, z, a, xh = (lax.axis_index(name) for name in AX)
    half = xh if keep else 1 - xh
    first = pl.multiple_of(half * HALF, HALF)
    blocks = rows.shape[0]
    samples = blocks * DEPTH
    copies = []
    for k in range(blocks):
        deep = pl.ds(k * DEPTH, DEPTH)
        copies.append(
            (
                pltpu.make_async_copy(cols_hbm.at[:, deep], cols.at[k], sem.at[0, k]),
                pltpu.make_async_copy(
                    rows_hbm.at[pl.ds(first, HALF), deep], rows.at[k], sem.at[1, k]
                ),
            )
        )
        for copy in copies[-1]:
            copy.start()
    final = pl.ds(place(N // 2), SUB)
    col_norm[...] = norm_ref[...]
    col_norm[final, :] = square_sums(last[0]) + square_sums(last[1])
    for k in range(blocks):
        for copy in copies[k]:
            copy.wait()
        source, start = divmod(k * DEPTH, samples // 2)
        cols[k, final, :] = last[source][:, start : start + DEPTH]
        part = lax.dot_general(
            rows[k],
            cols[k],
            (((1,), (1,)), ((), ())),
            preferred_element_type=jnp.float32,
        )
        norm = square_sums(rows[k])
        if k == 0:
            inner[...] = part
            row_norm[...] = norm
        else:
            inner[...] += part
            row_norm[...] += norm
    scale = live_ref[2 * y + xl, 2 * z + a].astype(jnp.float32)
    down = jnp.sum(row_norm[...], axis=1, keepdims=True)
    across = jnp.sum(col_norm[...].T, axis=0, keepdims=True)
    dist = down + across - 2.0 * inner[...]
    gram = jnp.exp(dist * (-2.0 / samples)) * scale
    base = pl.multiple_of(col_half(z, xh) * HALF, HALF) if keep else 0
    out_ref[:, pl.ds(base, HALF)] = gram.astype(jnp.bfloat16)


def gram_tile(keep, pair_live, rows, cols, col_norm, last):
    samples = cols.shape[1]
    width = 2 * HALF if keep else HALF
    operand = pltpu.VMEM((samples // DEPTH, HALF, DEPTH), jnp.bfloat16)
    return pl.pallas_call(
        functools.partial(gram_kernel, keep),
        out_shape=jax.ShapeDtypeStruct((HALF, width), jnp.bfloat16),
        in_specs=[
            pl.BlockSpec(memory_space=pltpu.SMEM),
            pl.BlockSpec(memory_space=pl.ANY),
            pl.BlockSpec(memory_space=pl.ANY),
            pl.BlockSpec(memory_space=pltpu.VMEM),
            pl.BlockSpec(memory_space=pltpu.VMEM),
            pl.BlockSpec(memory_space=pltpu.VMEM),
        ],
        out_specs=pl.BlockSpec(memory_space=pltpu.VMEM),
        scratch_shapes=[
            operand,
            operand,
            pltpu.VMEM((HALF, HALF), jnp.float32),
            pltpu.VMEM((HALF, 128), jnp.float32),
            pltpu.VMEM((HALF, 128), jnp.float32),
            pltpu.SemaphoreType.DMA((2, samples // DEPTH)),
        ],
        compiler_params=pltpu.CompilerParams(vmem_limit_bytes=56 * MIB),
        cost_estimate=pl.CostEstimate(
            flops=2 * HALF * HALF * samples,
            bytes_accessed=9 * MIB,
            transcendentals=HALF * HALF,
        ),
    )(pair_live, rows, cols, col_norm, *last)


def on_device(trajectories, pair_live):
    xl, z, xh = (lax.axis_index(name) for name in ("xl", "z", "xh"))

    def send(value, to):
        return lax.ppermute(value, AX, to)

    other = send(trajectories, swap_lag())
    early = send(trajectories, col_pairs(0))
    late = send(trajectories, col_pairs(1))
    early, other = lax.optimization_barrier((early, other))
    rows = jnp.where(
        xl == 0,
        jnp.concatenate([trajectories, other], axis=1),
        jnp.concatenate([other, trajectories], axis=1),
    )
    rows = lax.all_gather(rows, ("z", "a"), axis=0, tiled=True)

    steps, sources = [0], [early, late]
    up, down = [early, late], [early, late]
    for step in range(1, N // 2):
        up = [send(part, shift_y(1)) for part in up]
        down = [send(part, shift_y(-1)) for part in down]
        steps += [step, -step]
        sources += up + down
    cols, col_norm = in_order(steps, sources)
    last = [send(up[0], shift_y(1)), send(down[1], shift_y(-1))]

    given = send(gram_tile(False, pair_live, rows, cols, col_norm, last), swap_lag())
    kept = gram_tile(True, pair_live, rows, cols, col_norm, last)
    return lax.dynamic_update_slice(kept, given, (0, (1 - col_half(z, xh)) * HALF))


def solution(mesh):
    fine = Mesh(mesh.devices.reshape(N, 2, N, 2, 2), AX)
    return jax.shard_map(
        on_device,
        mesh=fine,
        in_specs=(P(("y", "xl", "z", "a"), "xh"), P()),
        out_specs=P(("y", "xl", "xh"), ("z", "a")),
        check_vma=False,
    )
```

```python
import functools

import jax
import jax.numpy as jnp
from jax import lax
from jax.experimental import pallas as pl
from jax.experimental.pallas import tpu as pltpu
from jax.sharding import Mesh
from jax.sharding import PartitionSpec as P

AX = ("y", "xl", "z", "a", "xh")
N = 8
SUB = 64
HALF = N * SUB
DEPTH = 1024
SHIFT = ((0, 4), (1, -1), (2, -2), (3, -3))
MIB = 1024 * 1024


def index(y, xl, z, a, xh):
    return (((y % N * 2 + xl) * N + z % N) * 2 + a) * 2 + xh


def pairs(target):
    every = [
        (y, xl, z, a, xh)
        for y in range(N)
        for xl in range(2)
        for z in range(N)
        for a in range(2)
        for xh in range(2)
    ]
    return [(index(*d), index(*target(*d))) for d in every]


def col_half(z, xh):
    return xh ^ (z >> 1 & 1)


def col_pairs(stage):
    def target(y, xl, z, a, half):
        part = col_half(y, z // 4)
        return y + SHIFT[z % 4][a], half ^ part ^ stage, y, xl, part

    return pairs(target)


def turn(step):
    return pairs(lambda y, xl, z, a, xh: (y + (-step if a else step), xl, z, a, xh))


def swap_lag():
    return pairs(lambda y, xl, z, a, xh: (y, xl, z, a, 1 - xh))


def square_sums(x):
    total = jnp.zeros((x.shape[0], 128), jnp.float32)
    for c in range(x.shape[1] // 128):
        part = x[:, c * 128 : (c + 1) * 128].astype(jnp.float32)
        total += part * part
    return total


def place(d):
    y, z, a = (lax.axis_index(name) for name in ("y", "z", "a"))
    o = (y - d * (1 - 2 * a) - z) & (N - 1)
    j = jnp.where(o < 4, 2 * o, (17 - 2 * o) & (N - 1))
    return pl.multiple_of(j * SUB, SUB)


def order_kernel(steps, *refs):
    count = len(steps)
    sources = refs[:count]
    cols, norm, held, sums, sem = refs[count:]
    loads = [
        pltpu.make_async_copy(source, held.at[i], sem.at[0, i])
        for i, source in enumerate(sources)
    ]
    for load in loads:
        load.start()
    stores = []
    for i, d in enumerate(steps):
        to = pl.ds(place(d), SUB)
        loads[i].wait()
        stores.append(pltpu.make_async_copy(held.at[i], cols.at[to, :], sem.at[1, i]))
        stores[-1].start()
        sums[i] = square_sums(held[i])
        stores.append(pltpu.make_async_copy(sums.at[i], norm.at[to, :], sem.at[2, i]))
        stores[-1].start()
    for store in stores:
        store.wait()


def in_order(steps, sources):
    samples = sources[0].shape[1]
    count = len(sources)
    return pl.pallas_call(
        functools.partial(order_kernel, steps),
        out_shape=(
            jax.ShapeDtypeStruct((HALF, samples), jnp.bfloat16),
            jax.ShapeDtypeStruct((HALF, 128), jnp.float32),
        ),
        in_specs=[pl.BlockSpec(memory_space=pl.ANY)] * count,
        out_specs=[pl.BlockSpec(memory_space=pl.ANY)] * 2,
        scratch_shapes=[
            pltpu.VMEM((count, SUB, samples), jnp.bfloat16),
            pltpu.VMEM((count, SUB, 128), jnp.float32),
            pltpu.SemaphoreType.DMA((3, count)),
        ],
        compiler_params=pltpu.CompilerParams(vmem_limit_bytes=56 * MIB),
        cost_estimate=pl.CostEstimate(
            flops=2 * count * SUB * samples,
            bytes_accessed=count * MIB,
            transcendentals=0,
        ),
    )(*sources)


def gram_kernel(keep, live_ref, rows_hbm, cols_hbm, norm_ref, *refs):
    last, out_ref = refs[:2], refs[2]
    rows, cols, inner, row_norm, col_norm, sem = refs[3:]
    y, xl, z, a, xh = (lax.axis_index(name) for name in AX)
    half = xh if keep else 1 - xh
    first = pl.multiple_of(half * HALF, HALF)
    blocks = rows.shape[0]
    samples = blocks * DEPTH
    copies = []
    for k in range(blocks):
        deep = pl.ds(k * DEPTH, DEPTH)
        copies.append(
            (
                pltpu.make_async_copy(cols_hbm.at[:, deep], cols.at[k], sem.at[0, k]),
                pltpu.make_async_copy(
                    rows_hbm.at[pl.ds(first, HALF), deep], rows.at[k], sem.at[1, k]
                ),
            )
        )
        for copy in copies[-1]:
            copy.start()
    part = SUB // 2
    final = place(N // 2)
    final = [pl.ds(pl.multiple_of(final + i * part, part), part) for i in range(2)]
    col_norm[...] = norm_ref[...]
    for to, source in zip(final, last):
        col_norm[to, :] = square_sums(source)
    for k in range(blocks):
        for copy in copies[k]:
            copy.wait()
        for to, source in zip(final, last):
            cols[k, to, :] = source[:, k * DEPTH : (k + 1) * DEPTH]
        product = lax.dot_general(
            rows[k],
            cols[k],
            (((1,), (1,)), ((), ())),
            preferred_element_type=jnp.float32,
        )
        norm = square_sums(rows[k])
        if k == 0:
            inner[...] = product
            row_norm[...] = norm
        else:
            inner[...] += product
            row_norm[...] += norm
    scale = live_ref[2 * y + xl, 2 * z + a].astype(jnp.float32)
    down = jnp.sum(row_norm[...], axis=1, keepdims=True)
    across = jnp.sum(col_norm[...].T, axis=0, keepdims=True)
    dist = down + across - 2.0 * inner[...]
    gram = jnp.exp(dist * (-2.0 / samples)) * scale
    base = pl.multiple_of(col_half(z, xh) * HALF, HALF) if keep else 0
    out_ref[:, pl.ds(base, HALF)] = gram.astype(jnp.bfloat16)


def gram_tile(keep, pair_live, rows, cols, col_norm, last):
    samples = cols.shape[1]
    width = 2 * HALF if keep else HALF
    operand = pltpu.VMEM((samples // DEPTH, HALF, DEPTH), jnp.bfloat16)
    return pl.pallas_call(
        functools.partial(gram_kernel, keep),
        out_shape=jax.ShapeDtypeStruct((HALF, width), jnp.bfloat16),
        in_specs=[
            pl.BlockSpec(memory_space=pltpu.SMEM),
            pl.BlockSpec(memory_space=pl.ANY),
            pl.BlockSpec(memory_space=pl.ANY),
            pl.BlockSpec(memory_space=pltpu.VMEM),
            pl.BlockSpec(memory_space=pltpu.VMEM),
            pl.BlockSpec(memory_space=pltpu.VMEM),
        ],
        out_specs=pl.BlockSpec(memory_space=pltpu.VMEM),
        scratch_shapes=[
            operand,
            operand,
            pltpu.VMEM((HALF, HALF), jnp.float32),
            pltpu.VMEM((HALF, 128), jnp.float32),
            pltpu.VMEM((HALF, 128), jnp.float32),
            pltpu.SemaphoreType.DMA((2, samples // DEPTH)),
        ],
        compiler_params=pltpu.CompilerParams(vmem_limit_bytes=56 * MIB),
        cost_estimate=pl.CostEstimate(
            flops=2 * HALF * HALF * samples,
            bytes_accessed=9 * MIB,
            transcendentals=HALF * HALF,
        ),
    )(pair_live, rows, cols, col_norm, *last)


def on_device(trajectories, pair_live):
    xl, z, xh = (lax.axis_index(name) for name in ("xl", "z", "xh"))

    def send(value, to):
        return lax.ppermute(value, AX, to)

    other = send(trajectories, swap_lag())
    early = send(trajectories, col_pairs(0))
    late = send(trajectories, col_pairs(1))
    early, other = lax.optimization_barrier((early, other))
    rows = jnp.where(
        xl == 0,
        jnp.concatenate([trajectories, other], axis=1),
        jnp.concatenate([other, trajectories], axis=1),
    )
    rows = lax.all_gather(rows, ("z", "a"), axis=0, tiled=True)

    first = second = jnp.concatenate([early, late], axis=1)
    steps, sources = [0], [first]
    for step in range(1, N // 2):
        first, second = send(first, turn(1)), send(second, turn(-1))
        steps += [step, -step]
        sources += [first, second]
    cols, col_norm = in_order(steps, sources)
    part = SUB // 2
    last = [send(first[:part], turn(1)), send(second[part:], turn(-1))]

    given = send(gram_tile(False, pair_live, rows, cols, col_norm, last), swap_lag())
    kept = gram_tile(True, pair_live, rows, cols, col_norm, last)
    return lax.dynamic_update_slice(kept, given, (0, (1 - col_half(z, xh)) * HALF))


def solution(mesh):
    fine = Mesh(mesh.devices.reshape(N, 2, N, 2, 2), AX)
    return jax.shard_map(
        on_device,
        mesh=fine,
        in_specs=(P(("y", "xl", "z", "a"), "xh"), P()),
        out_specs=P(("y", "xl", "xh"), ("z", "a")),
        check_vma=False,
    )
```

```python
import functools

import jax
import jax.numpy as jnp
from jax import lax
from jax.experimental import pallas as pl
from jax.experimental.pallas import tpu as pltpu
from jax.sharding import Mesh
from jax.sharding import PartitionSpec as P

AX = ("y", "xl", "z", "a", "xh")
N = 8
SUB = 64
HALF = N * SUB
DEPTH = 1024
SHIFT = ((0, 4), (1, -1), (2, -2), (3, -3))
MIB = 1024 * 1024


def index(y, xl, z, a, xh):
    return (((y % N * 2 + xl) * N + z % N) * 2 + a) * 2 + xh


def pairs(target):
    every = [
        (y, xl, z, a, xh)
        for y in range(N)
        for xl in range(2)
        for z in range(N)
        for a in range(2)
        for xh in range(2)
    ]
    return [(index(*d), index(*target(*d))) for d in every]


def col_half(z, xh):
    return xh ^ (z >> 1 & 1)


def col_pairs(stage):
    def target(y, xl, z, a, half):
        part = col_half(y, z // 4)
        return y + SHIFT[z % 4][a], half ^ part ^ stage, y, xl, part

    return pairs(target)


def shift_y(step):
    return pairs(lambda y, xl, z, a, xh: (y + step, xl, z, a, xh))


def swap_lag():
    return pairs(lambda y, xl, z, a, xh: (y, xl, z, a, 1 - xh))


def square_sums(x):
    total = jnp.zeros((x.shape[0], 128), jnp.float32)
    for c in range(x.shape[1] // 128):
        part = x[:, c * 128 : (c + 1) * 128].astype(jnp.float32)
        total += part * part
    return total


def place(d):
    o = (lax.axis_index("y") - d - lax.axis_index("z")) & (N - 1)
    j = jnp.where(o < 4, 2 * o, (17 - 2 * o) & (N - 1))
    return pl.multiple_of(j * SUB, SUB)


def gram_kernel(keep, steps, live_ref, rows_hbm, *refs):
    chunks, out_ref = refs[: 2 * len(steps)], refs[2 * len(steps)]
    rows, cols, inner, row_norm, col_norm, sem = refs[2 * len(steps) + 1 :]
    y, xl, z, a, xh = (lax.axis_index(name) for name in AX)
    half = xh if keep else 1 - xh
    first = pl.multiple_of(half * HALF, HALF)
    blocks = rows.shape[0]
    samples = blocks * DEPTH
    places = [pl.ds(place(d), SUB) for d in steps]
    copies = []
    for k in range(blocks):
        copies.append(
            [
                pltpu.make_async_copy(
                    rows_hbm.at[pl.ds(first, HALF), pl.ds(k * DEPTH, DEPTH)],
                    rows.at[k],
                    sem.at[k, len(steps)],
                )
            ]
        )
        part, start = divmod(k * DEPTH, samples // 2)
        for i, to in enumerate(places):
            copies[k].append(
                pltpu.make_async_copy(
                    chunks[2 * i + part].at[:, pl.ds(start, DEPTH)],
                    cols.at[k, to, :],
                    sem.at[k, i],
                )
            )
        for copy in copies[k]:
            copy.start()
    for k in range(blocks):
        for copy in copies[k]:
            copy.wait()
        product = lax.dot_general(
            rows[k], cols[k], (((1,), (1,)), ((), ())), preferred_element_type=jnp.float32
        )
        down, across = square_sums(rows[k]), square_sums(cols[k])
        if k == 0:
            inner[...] = product
            row_norm[...] = down
            col_norm[...] = across
        else:
            inner[...] += product
            row_norm[...] += down
            col_norm[...] += across
    scale = live_ref[2 * y + xl, 2 * z + a].astype(jnp.float32)
    down = jnp.sum(row_norm[...], axis=1, keepdims=True)
    across = jnp.sum(col_norm[...].T, axis=0, keepdims=True)
    dist = down + across - 2.0 * inner[...]
    gram = jnp.exp(dist * (-2.0 / samples)) * scale
    base = pl.multiple_of(col_half(z, xh) * HALF, HALF) if keep else 0
    out_ref[:, pl.ds(base, HALF)] = gram.astype(jnp.bfloat16)


def gram_tile(keep, pair_live, rows, steps, chunks):
    samples = rows.shape[1]
    width = 2 * HALF if keep else HALF
    operand = pltpu.VMEM((samples // DEPTH, HALF, DEPTH), jnp.bfloat16)
    return pl.pallas_call(
        functools.partial(gram_kernel, keep, steps),
        out_shape=jax.ShapeDtypeStruct((HALF, width), jnp.bfloat16),
        in_specs=[pl.BlockSpec(memory_space=pltpu.SMEM)]
        + [pl.BlockSpec(memory_space=pl.ANY)] * (1 + len(chunks)),
        out_specs=pl.BlockSpec(memory_space=pltpu.VMEM),
        scratch_shapes=[
            operand,
            operand,
            pltpu.VMEM((HALF, HALF), jnp.float32),
            pltpu.VMEM((HALF, 128), jnp.float32),
            pltpu.VMEM((HALF, 128), jnp.float32),
            pltpu.SemaphoreType.DMA((samples // DEPTH, N + 1)),
        ],
        compiler_params=pltpu.CompilerParams(vmem_limit_bytes=56 * MIB),
        cost_estimate=pl.CostEstimate(
            flops=2 * HALF * HALF * samples,
            bytes_accessed=9 * MIB,
            transcendentals=HALF * HALF,
        ),
    )(pair_live, rows, *chunks)


def on_device(trajectories, pair_live):
    xl, z, xh = (lax.axis_index(name) for name in ("xl", "z", "xh"))

    def send(value, to):
        return lax.ppermute(value, AX, to)

    other = send(trajectories, swap_lag())
    early = send(trajectories, col_pairs(0))
    late = send(trajectories, col_pairs(1))
    early, other = lax.optimization_barrier((early, other))
    rows = jnp.where(
        xl == 0,
        jnp.concatenate([trajectories, other], axis=1),
        jnp.concatenate([other, trajectories], axis=1),
    )
    rows = lax.all_gather(rows, ("z", "a"), axis=0, tiled=True)

    steps, chunks = [0], [early, late]
    up, down = [early, late], [early, late]
    for step in range(1, N // 2):
        up = [send(part, shift_y(1)) for part in up]
        down = [send(part, shift_y(-1)) for part in down]
        steps += [step, -step]
        chunks += up + down
    steps.append(N // 2)
    chunks += [send(up[0], shift_y(1)), send(down[1], shift_y(-1))]

    given = send(gram_tile(False, pair_live, rows, steps, chunks), swap_lag())
    kept = gram_tile(True, pair_live, rows, steps, chunks)
    return lax.dynamic_update_slice(kept, given, (0, (1 - col_half(z, xh)) * HALF))


def solution(mesh):
    fine = Mesh(mesh.devices.reshape(N, 2, N, 2, 2), AX)
    return jax.shard_map(
        on_device,
        mesh=fine,
        in_specs=(P(("y", "xl", "z", "a"), "xh"), P()),
        out_specs=P(("y", "xl", "xh"), ("z", "a")),
        check_vma=False,
    )
```

```python
import functools

import jax
import jax.numpy as jnp
from jax import lax
from jax.experimental import pallas as pl
from jax.experimental.pallas import tpu as pltpu
from jax.sharding import Mesh
from jax.sharding import PartitionSpec as P

AX = ("y", "xl", "z", "a", "xh")
N = 8
SUB = 64
HALF = N * SUB
DEPTH = 1024
SHIFT = ((0, 4), (1, -1), (2, -2), (3, -3))
MIB = 1024 * 1024


def index(y, xl, z, a, xh):
    return (((y % N * 2 + xl) * N + z % N) * 2 + a) * 2 + xh


def pairs(target):
    every = [
        (y, xl, z, a, xh)
        for y in range(N)
        for xl in range(2)
        for z in range(N)
        for a in range(2)
        for xh in range(2)
    ]
    return [(index(*d), index(*target(*d))) for d in every]


def col_half(z, xh):
    return xh ^ (z >> 1 & 1)


def col_pairs(stage):
    def target(y, xl, z, a, half):
        part = col_half(y, z // 4)
        return y + SHIFT[z % 4][a], half ^ part ^ stage, y, xl, part

    return pairs(target)


def shift_y(step):
    return pairs(lambda y, xl, z, a, xh: (y + step, xl, z, a, xh))


def swap_lag():
    return pairs(lambda y, xl, z, a, xh: (y, xl, z, a, 1 - xh))


def square_sums(x):
    total = jnp.zeros((x.shape[0], 128), jnp.float32)
    for c in range(x.shape[1] // 128):
        part = x[:, c * 128 : (c + 1) * 128].astype(jnp.float32)
        total += part * part
    return total


def place(d):
    o = (lax.axis_index("y") - d - lax.axis_index("z")) & (N - 1)
    j = jnp.where(o < 4, 2 * o, (17 - 2 * o) & (N - 1))
    return pl.multiple_of(j * SUB, SUB)


def gram_kernel(keep, steps, live_ref, rows_hbm, *refs):
    chunks, out_ref = refs[: 2 * len(steps)], refs[2 * len(steps)]
    rows, cols, inner, row_norm, col_norm, sem = refs[2 * len(steps) + 1 :]
    y, xl, z, a, xh = (lax.axis_index(name) for name in AX)
    half = xh if keep else 1 - xh
    first = pl.multiple_of(half * HALF, HALF)
    blocks = rows.shape[0]
    samples = blocks * DEPTH
    places = [pl.ds(place(d), SUB) for d in steps]
    copies = []
    for k in range(blocks):
        copies.append(
            [
                pltpu.make_async_copy(
                    rows_hbm.at[pl.ds(first, HALF), pl.ds(k * DEPTH, DEPTH)],
                    rows.at[k],
                    sem.at[k, len(steps)],
                )
            ]
        )
        part, start = divmod(k * DEPTH, samples // 2)
        for i, to in enumerate(places):
            copies[k].append(
                pltpu.make_async_copy(
                    chunks[2 * i + part].at[:, pl.ds(start, DEPTH)],
                    cols.at[k, to, :],
                    sem.at[k, i],
                )
            )
        for copy in copies[k]:
            copy.start()
    for k in range(blocks):
        for copy in copies[k]:
            copy.wait()
        product = lax.dot_general(
            rows[k], cols[k], (((1,), (1,)), ((), ())), preferred_element_type=jnp.float32
        )
        down, across = square_sums(rows[k]), square_sums(cols[k])
        if k == 0:
            inner[...] = product
            row_norm[...] = down
            col_norm[...] = across
        else:
            inner[...] += product
            row_norm[...] += down
            col_norm[...] += across
    scale = live_ref[2 * y + xl, 2 * z + a].astype(jnp.float32)
    down = jnp.sum(row_norm[...], axis=1, keepdims=True)
    across = jnp.sum(col_norm[...].T, axis=0, keepdims=True)
    dist = down + across - 2.0 * inner[...]
    gram = jnp.exp(dist * (-2.0 / samples)) * scale
    base = pl.multiple_of(col_half(z, xh) * HALF, HALF) if keep else 0
    out_ref[:, pl.ds(base, HALF)] = gram.astype(jnp.bfloat16)


def gram_tile(keep, pair_live, rows, steps, chunks):
    samples = rows.shape[1]
    width = 2 * HALF if keep else HALF
    operand = pltpu.VMEM((samples // DEPTH, HALF, DEPTH), jnp.bfloat16)
    return pl.pallas_call(
        functools.partial(gram_kernel, keep, steps),
        out_shape=jax.ShapeDtypeStruct((HALF, width), jnp.bfloat16),
        in_specs=[pl.BlockSpec(memory_space=pltpu.SMEM)]
        + [pl.BlockSpec(memory_space=pl.ANY)] * (1 + len(chunks)),
        out_specs=pl.BlockSpec(memory_space=pltpu.VMEM),
        scratch_shapes=[
            operand,
            operand,
            pltpu.VMEM((HALF, HALF), jnp.float32),
            pltpu.VMEM((HALF, 128), jnp.float32),
            pltpu.VMEM((HALF, 128), jnp.float32),
            pltpu.SemaphoreType.DMA((samples // DEPTH, N + 1)),
        ],
        compiler_params=pltpu.CompilerParams(vmem_limit_bytes=56 * MIB),
        cost_estimate=pl.CostEstimate(
            flops=2 * HALF * HALF * samples,
            bytes_accessed=9 * MIB,
            transcendentals=HALF * HALF,
        ),
    )(pair_live, rows, *chunks)


def on_device(trajectories, pair_live):
    xl, z, xh = (lax.axis_index(name) for name in ("xl", "z", "xh"))

    def send(value, to):
        return lax.ppermute(value, AX, to)

    other = send(trajectories, swap_lag())
    early = send(trajectories, col_pairs(0))
    late = send(trajectories, col_pairs(1))
    early, other = lax.optimization_barrier((early, other))
    rows = jnp.where(
        xl == 0,
        jnp.concatenate([trajectories, other], axis=1),
        jnp.concatenate([other, trajectories], axis=1),
    )
    rows = lax.all_gather(rows, ("z", "a"), axis=0, tiled=True)

    above, below = send(early, shift_y(1)), send(early, shift_y(-1))
    above, below, late = lax.optimization_barrier((above, below, late))
    up = [above, send(late, shift_y(1))]
    down = [below, send(late, shift_y(-1))]
    steps, chunks = [0, 1, -1], [early, late, *up, *down]
    for step in range(2, N // 2):
        up = [send(part, shift_y(1)) for part in up]
        down = [send(part, shift_y(-1)) for part in down]
        steps += [step, -step]
        chunks += up + down
    steps.append(N // 2)
    chunks += [send(up[0], shift_y(1)), send(down[1], shift_y(-1))]

    given = send(gram_tile(False, pair_live, rows, steps, chunks), swap_lag())
    kept = gram_tile(True, pair_live, rows, steps, chunks)
    return lax.dynamic_update_slice(kept, given, (0, (1 - col_half(z, xh)) * HALF))


def solution(mesh):
    fine = Mesh(mesh.devices.reshape(N, 2, N, 2, 2), AX)
    return jax.shard_map(
        on_device,
        mesh=fine,
        in_specs=(P(("y", "xl", "z", "a"), "xh"), P()),
        out_specs=P(("y", "xl", "xh"), ("z", "a")),
        check_vma=False,
    )
```

```python
import functools

import jax
import jax.numpy as jnp
from jax import lax
from jax.experimental import pallas as pl
from jax.experimental.pallas import tpu as pltpu
from jax.sharding import Mesh
from jax.sharding import PartitionSpec as P

AX = ("y", "xl", "z", "a", "xh")
N = 8
SUB = 64
HALF = N * SUB
DEPTH = 1024
SHIFT = ((0, 4), (1, -1), (2, -2), (3, -3))
MIB = 1024 * 1024


def index(y, xl, z, a, xh):
    return (((y % N * 2 + xl) * N + z % N) * 2 + a) * 2 + xh


def pairs(target):
    every = [
        (y, xl, z, a, xh)
        for y in range(N)
        for xl in range(2)
        for z in range(N)
        for a in range(2)
        for xh in range(2)
    ]
    return [(index(*d), index(*target(*d))) for d in every]


def col_half(z, xh):
    return xh ^ (z >> 1 & 1)


def col_pairs(stage):
    def target(y, xl, z, a, half):
        part = col_half(y, z // 4)
        return y + SHIFT[z % 4][a], half ^ part ^ stage, y, xl, part

    return pairs(target)


def shift_y(step):
    return pairs(lambda y, xl, z, a, xh: (y + step, xl, z, a, xh))


def swap_lag():
    return pairs(lambda y, xl, z, a, xh: (y, xl, z, a, 1 - xh))


def square_sums(x):
    total = jnp.zeros((x.shape[0], 128), jnp.float32)
    for c in range(x.shape[1] // 128):
        part = x[:, c * 128 : (c + 1) * 128].astype(jnp.float32)
        total += part * part
    return total


def place(d):
    o = (lax.axis_index("y") - d - lax.axis_index("z")) & (N - 1)
    j = jnp.where(o < 4, 2 * o, (17 - 2 * o) & (N - 1))
    return pl.multiple_of(j * SUB, SUB)


def gram_kernel(keep, steps, live_ref, rows_hbm, *refs):
    chunks, out_ref = refs[: 2 * len(steps)], refs[2 * len(steps)]
    rows, cols, inner, row_norm, col_norm, sem = refs[2 * len(steps) + 1 :]
    y, xl, z, a, xh = (lax.axis_index(name) for name in AX)
    half = xh if keep else 1 - xh
    first = pl.multiple_of(half * HALF, HALF)
    blocks = rows.shape[0]
    samples = blocks * DEPTH
    places = [pl.ds(place(d), SUB) for d in steps]
    copies = []
    for k in range(blocks):
        copies.append(
            [
                pltpu.make_async_copy(
                    rows_hbm.at[pl.ds(first, HALF), pl.ds(k * DEPTH, DEPTH)],
                    rows.at[k],
                    sem.at[k, len(steps)],
                )
            ]
        )
        part, start = divmod(k * DEPTH, samples // 2)
        for i, to in enumerate(places):
            copies[k].append(
                pltpu.make_async_copy(
                    chunks[2 * i + part].at[:, pl.ds(start, DEPTH)],
                    cols.at[k, to, :],
                    sem.at[k, i],
                )
            )
        for copy in copies[k]:
            copy.start()
    for k in range(blocks):
        for copy in copies[k]:
            copy.wait()
        product = lax.dot_general(
            rows[k], cols[k], (((1,), (1,)), ((), ())), preferred_element_type=jnp.float32
        )
        down, across = square_sums(rows[k]), square_sums(cols[k])
        if k == 0:
            inner[...] = product
            row_norm[...] = down
            col_norm[...] = across
        else:
            inner[...] += product
            row_norm[...] += down
            col_norm[...] += across
    scale = live_ref[2 * y + xl, 2 * z + a].astype(jnp.float32)
    down = jnp.sum(row_norm[...], axis=1, keepdims=True)
    across = jnp.sum(col_norm[...].T, axis=0, keepdims=True)
    dist = down + across - 2.0 * inner[...]
    gram = jnp.exp(dist * (-2.0 / samples)) * scale
    base = pl.multiple_of(col_half(z, xh) * HALF, HALF) if keep else 0
    out_ref[:, pl.ds(base, HALF)] = gram.astype(jnp.bfloat16)


def gram_tile(keep, pair_live, rows, steps, chunks):
    samples = rows.shape[1]
    width = 2 * HALF if keep else HALF
    operand = pltpu.VMEM((samples // DEPTH, HALF, DEPTH), jnp.bfloat16)
    return pl.pallas_call(
        functools.partial(gram_kernel, keep, steps),
        out_shape=jax.ShapeDtypeStruct((HALF, width), jnp.bfloat16),
        in_specs=[pl.BlockSpec(memory_space=pltpu.SMEM)]
        + [pl.BlockSpec(memory_space=pl.ANY)] * (1 + len(chunks)),
        out_specs=pl.BlockSpec(memory_space=pltpu.VMEM),
        scratch_shapes=[
            operand,
            operand,
            pltpu.VMEM((HALF, HALF), jnp.float32),
            pltpu.VMEM((HALF, 128), jnp.float32),
            pltpu.VMEM((HALF, 128), jnp.float32),
            pltpu.SemaphoreType.DMA((samples // DEPTH, N + 1)),
        ],
        compiler_params=pltpu.CompilerParams(vmem_limit_bytes=56 * MIB),
        cost_estimate=pl.CostEstimate(
            flops=2 * HALF * HALF * samples,
            bytes_accessed=9 * MIB,
            transcendentals=HALF * HALF,
        ),
    )(pair_live, rows, *chunks)


def on_device(trajectories, pair_live):
    xl, z, xh = (lax.axis_index(name) for name in ("xl", "z", "xh"))

    def send(value, to):
        return lax.ppermute(value, AX, to)

    other = send(trajectories, swap_lag())
    early = send(trajectories, col_pairs(0))
    late = send(trajectories, col_pairs(1))
    early, late, other = lax.optimization_barrier((early, late, other))
    rows = jnp.where(
        xl == 0,
        jnp.concatenate([trajectories, other], axis=1),
        jnp.concatenate([other, trajectories], axis=1),
    )
    rows = lax.all_gather(rows, ("z", "a"), axis=0, tiled=True)

    steps, chunks = [0], [early, late]
    up, down = [early, late], [early, late]
    for step in range(1, N // 2):
        up = [send(part, shift_y(1)) for part in up]
        down = [send(part, shift_y(-1)) for part in down]
        steps += [step, -step]
        chunks += up + down
    steps.append(N // 2)
    chunks += [send(up[0], shift_y(1)), send(down[1], shift_y(-1))]

    given = send(gram_tile(False, pair_live, rows, steps, chunks), swap_lag())
    kept = gram_tile(True, pair_live, rows, steps, chunks)
    return lax.dynamic_update_slice(kept, given, (0, (1 - col_half(z, xh)) * HALF))


def solution(mesh):
    fine = Mesh(mesh.devices.reshape(N, 2, N, 2, 2), AX)
    return jax.shard_map(
        on_device,
        mesh=fine,
        in_specs=(P(("y", "xl", "z", "a"), "xh"), P()),
        out_specs=P(("y", "xl", "xh"), ("z", "a")),
        check_vma=False,
    )
```

```python
import functools

import jax
import jax.numpy as jnp
from jax import lax
from jax.experimental import pallas as pl
from jax.experimental.pallas import tpu as pltpu
from jax.sharding import Mesh
from jax.sharding import PartitionSpec as P

AX = ("y", "xl", "z", "a", "xh")
N = 8
SUB = 64
HALF = N * SUB
DEPTH = 1024
SHIFT = ((0, 4), (1, -1), (2, -2), (3, -3))
MIB = 1024 * 1024


def index(y, xl, z, a, xh):
    return (((y % N * 2 + xl) * N + z % N) * 2 + a) * 2 + xh


def pairs(target):
    every = [
        (y, xl, z, a, xh)
        for y in range(N)
        for xl in range(2)
        for z in range(N)
        for a in range(2)
        for xh in range(2)
    ]
    return [(index(*d), index(*target(*d))) for d in every]


def col_half(z, xh):
    return xh ^ (z >> 1 & 1)


def col_pairs(stage):
    def target(y, xl, z, a, half):
        part = col_half(y, z // 4)
        return y + SHIFT[z % 4][a], half ^ part ^ stage, y, xl, part

    return pairs(target)


def shift_y(step):
    return pairs(lambda y, xl, z, a, xh: (y + step, xl, z, a, xh))


def swap_lag():
    return pairs(lambda y, xl, z, a, xh: (y, xl, z, a, 1 - xh))


def square_sums(x):
    total = jnp.zeros((x.shape[0], 128), jnp.float32)
    for c in range(x.shape[1] // 128):
        part = x[:, c * 128 : (c + 1) * 128].astype(jnp.float32)
        total += part * part
    return total


def place(d):
    o = (lax.axis_index("y") - d - lax.axis_index("z")) & (N - 1)
    j = jnp.where(o < 4, 2 * o, (17 - 2 * o) & (N - 1))
    return pl.multiple_of(j * SUB, SUB)


def gram_kernel(keep, steps, live_ref, rows_hbm, *refs):
    chunks, out_ref = refs[: 2 * len(steps)], refs[2 * len(steps)]
    rows, cols, inner, row_norm, col_norm, sem = refs[2 * len(steps) + 1 :]
    y, xl, z, a, xh = (lax.axis_index(name) for name in AX)
    half = xh if keep else 1 - xh
    first = pl.multiple_of(half * HALF, HALF)
    blocks = rows.shape[0]
    samples = blocks * DEPTH
    places = [pl.ds(place(d), SUB) for d in steps]
    copies = []
    for k in range(blocks):
        part, start = divmod(k * DEPTH, samples // 2)
        deep = pl.multiple_of((part ^ xl) * (samples // 2) + start, DEPTH)
        copies.append(
            [
                pltpu.make_async_copy(
                    rows_hbm.at[pl.ds(first, HALF), pl.ds(deep, DEPTH)],
                    rows.at[k],
                    sem.at[k, len(steps)],
                )
            ]
        )
        for i, to in enumerate(places):
            copies[k].append(
                pltpu.make_async_copy(
                    chunks[2 * i + part].at[:, pl.ds(start, DEPTH)],
                    cols.at[k, to, :],
                    sem.at[k, i],
                )
            )
        for copy in copies[k]:
            copy.start()
    for k in range(blocks):
        for copy in copies[k]:
            copy.wait()
        product = lax.dot_general(
            rows[k], cols[k], (((1,), (1,)), ((), ())), preferred_element_type=jnp.float32
        )
        down, across = square_sums(rows[k]), square_sums(cols[k])
        if k == 0:
            inner[...] = product
            row_norm[...] = down
            col_norm[...] = across
        else:
            inner[...] += product
            row_norm[...] += down
            col_norm[...] += across
    scale = live_ref[2 * y + xl, 2 * z + a].astype(jnp.float32)
    down = jnp.sum(row_norm[...], axis=1, keepdims=True)
    across = jnp.sum(col_norm[...].T, axis=0, keepdims=True)
    dist = down + across - 2.0 * inner[...]
    gram = jnp.exp(dist * (-2.0 / samples)) * scale
    base = pl.multiple_of(col_half(z, xh) * HALF, HALF) if keep else 0
    out_ref[:, pl.ds(base, HALF)] = gram.astype(jnp.bfloat16)


def gram_tile(keep, pair_live, rows, steps, chunks):
    samples = rows.shape[1]
    width = 2 * HALF if keep else HALF
    operand = pltpu.VMEM((samples // DEPTH, HALF, DEPTH), jnp.bfloat16)
    return pl.pallas_call(
        functools.partial(gram_kernel, keep, steps),
        out_shape=jax.ShapeDtypeStruct((HALF, width), jnp.bfloat16),
        in_specs=[pl.BlockSpec(memory_space=pltpu.SMEM)]
        + [pl.BlockSpec(memory_space=pl.ANY)] * (1 + len(chunks)),
        out_specs=pl.BlockSpec(memory_space=pltpu.VMEM),
        scratch_shapes=[
            operand,
            operand,
            pltpu.VMEM((HALF, HALF), jnp.float32),
            pltpu.VMEM((HALF, 128), jnp.float32),
            pltpu.VMEM((HALF, 128), jnp.float32),
            pltpu.SemaphoreType.DMA((samples // DEPTH, N + 1)),
        ],
        compiler_params=pltpu.CompilerParams(vmem_limit_bytes=56 * MIB),
        cost_estimate=pl.CostEstimate(
            flops=2 * HALF * HALF * samples,
            bytes_accessed=9 * MIB,
            transcendentals=HALF * HALF,
        ),
    )(pair_live, rows, *chunks)


def on_device(trajectories, pair_live):
    z, xh = lax.axis_index("z"), lax.axis_index("xh")

    def send(value, to):
        return lax.ppermute(value, AX, to)

    other = send(trajectories, swap_lag())
    early = send(trajectories, col_pairs(0))
    late = send(trajectories, col_pairs(1))
    early, late, other = lax.optimization_barrier((early, late, other))
    rows = jnp.concatenate([trajectories, other], axis=1)
    rows = lax.all_gather(rows, ("z", "a"), axis=0, tiled=True)

    steps, chunks = [0], [early, late]
    up, down = [early, late], [early, late]
    for step in range(1, N // 2):
        up = [send(part, shift_y(1)) for part in up]
        down = [send(part, shift_y(-1)) for part in down]
        steps += [step, -step]
        chunks += up + down
    steps.append(N // 2)
    chunks += [send(up[0], shift_y(1)), send(down[1], shift_y(-1))]

    given = send(gram_tile(False, pair_live, rows, steps, chunks), swap_lag())
    kept = gram_tile(True, pair_live, rows, steps, chunks)
    return lax.dynamic_update_slice(kept, given, (0, (1 - col_half(z, xh)) * HALF))


def solution(mesh):
    fine = Mesh(mesh.devices.reshape(N, 2, N, 2, 2), AX)
    return jax.shard_map(
        on_device,
        mesh=fine,
        in_specs=(P(("y", "xl", "z", "a"), "xh"), P()),
        out_specs=P(("y", "xl", "xh"), ("z", "a")),
        check_vma=False,
    )
```

```python
import functools

import jax
import jax.numpy as jnp
from jax import lax
from jax.experimental import pallas as pl
from jax.experimental.pallas import tpu as pltpu
from jax.sharding import Mesh
from jax.sharding import PartitionSpec as P

AX = ("y", "xl", "z", "a", "xh")
N = 8
SUB = 64
HALF = N * SUB
DEPTH = 1024
SHIFT = ((0, 4), (1, -1), (2, -2), (3, -3))
MIB = 1024 * 1024


def index(y, xl, z, a, xh):
    return (((y % N * 2 + xl) * N + z % N) * 2 + a) * 2 + xh


def pairs(target):
    every = [
        (y, xl, z, a, xh)
        for y in range(N)
        for xl in range(2)
        for z in range(N)
        for a in range(2)
        for xh in range(2)
    ]
    return [(index(*d), index(*target(*d))) for d in every]


def col_half(z, xh):
    return xh ^ (z >> 1 & 1)


def col_pairs(stage):
    def target(y, xl, z, a, half):
        part = col_half(y, z // 4)
        return y + SHIFT[z % 4][a], half ^ part ^ stage, y, xl, part

    return pairs(target)


def shift_y(step):
    return pairs(lambda y, xl, z, a, xh: (y + step, xl, z, a, xh))


def swap_lag():
    return pairs(lambda y, xl, z, a, xh: (y, xl, z, a, 1 - xh))


def square_sums(x):
    total = jnp.zeros((x.shape[0], 128), jnp.float32)
    for c in range(x.shape[1] // 128):
        part = x[:, c * 128 : (c + 1) * 128].astype(jnp.float32)
        total += part * part
    return total


def place(d):
    o = (lax.axis_index("y") - d - lax.axis_index("z")) & (N - 1)
    j = jnp.where(o < 4, 2 * o, (17 - 2 * o) & (N - 1))
    return pl.multiple_of(j * SUB, SUB)


def gram_kernel(keep, steps, live_ref, rows_hbm, *refs):
    chunks, out_ref = refs[: 2 * len(steps)], refs[2 * len(steps)]
    rows, cols, inner, row_norm, col_norm, sem = refs[2 * len(steps) + 1 :]
    y, xl, z, a, xh = (lax.axis_index(name) for name in AX)
    half = xh if keep else 1 - xh
    first = pl.multiple_of(half * HALF, HALF)
    blocks = rows.shape[0]
    samples = blocks * DEPTH
    places = [pl.ds(place(d), SUB) for d in steps]
    copies = []
    for k in range(blocks):
        part, start = divmod(k * DEPTH, samples // 2)
        deep = pl.multiple_of((part ^ xl) * (samples // 2) + start, DEPTH)
        copies.append(
            [
                pltpu.make_async_copy(
                    rows_hbm.at[pl.ds(first, HALF), pl.ds(deep, DEPTH)],
                    rows.at[k],
                    sem.at[k, len(steps)],
                )
            ]
        )
        for i, to in enumerate(places):
            copies[k].append(
                pltpu.make_async_copy(
                    chunks[2 * i + part].at[:, pl.ds(start, DEPTH)],
                    cols.at[k, to, :],
                    sem.at[k, i],
                )
            )
        for copy in copies[k]:
            copy.start()
    for k in range(blocks):
        for copy in copies[k]:
            copy.wait()
        product = lax.dot_general(
            rows[k], cols[k], (((1,), (1,)), ((), ())), preferred_element_type=jnp.float32
        )
        down, across = square_sums(rows[k]), square_sums(cols[k])
        if k == 0:
            inner[...] = product
            row_norm[...] = down
            col_norm[...] = across
        else:
            inner[...] += product
            row_norm[...] += down
            col_norm[...] += across
    scale = live_ref[2 * y + xl, 2 * z + a].astype(jnp.float32)
    down = jnp.sum(row_norm[...], axis=1, keepdims=True)
    across = jnp.sum(col_norm[...].T, axis=0, keepdims=True)
    dist = down + across - 2.0 * inner[...]
    gram = jnp.exp(dist * (-2.0 / samples)) * scale
    base = pl.multiple_of(col_half(z, xh) * HALF, HALF) if keep else 0
    out_ref[:, pl.ds(base, HALF)] = gram.astype(jnp.bfloat16)


def gram_tile(keep, pair_live, rows, steps, chunks):
    samples = rows.shape[1]
    width = 2 * HALF if keep else HALF
    operand = pltpu.VMEM((samples // DEPTH, HALF, DEPTH), jnp.bfloat16)
    return pl.pallas_call(
        functools.partial(gram_kernel, keep, steps),
        out_shape=jax.ShapeDtypeStruct((HALF, width), jnp.bfloat16),
        in_specs=[pl.BlockSpec(memory_space=pltpu.SMEM)]
        + [pl.BlockSpec(memory_space=pl.ANY)] * (1 + len(chunks)),
        out_specs=pl.BlockSpec(memory_space=pltpu.VMEM),
        scratch_shapes=[
            operand,
            operand,
            pltpu.VMEM((HALF, HALF), jnp.float32),
            pltpu.VMEM((HALF, 128), jnp.float32),
            pltpu.VMEM((HALF, 128), jnp.float32),
            pltpu.SemaphoreType.DMA((samples // DEPTH, N + 1)),
        ],
        compiler_params=pltpu.CompilerParams(vmem_limit_bytes=56 * MIB),
        cost_estimate=pl.CostEstimate(
            flops=2 * HALF * HALF * samples,
            bytes_accessed=9 * MIB,
            transcendentals=HALF * HALF,
        ),
    )(pair_live, rows, *chunks)


def on_device(trajectories, pair_live):
    z, xh = lax.axis_index("z"), lax.axis_index("xh")

    def send(value, to):
        return lax.ppermute(value, AX, to)

    other = send(trajectories, swap_lag())
    early = send(trajectories, col_pairs(0))
    late = send(trajectories, col_pairs(1))
    early, other = lax.optimization_barrier((early, other))
    rows = jnp.concatenate([trajectories, other], axis=1)
    rows = lax.all_gather(rows, ("z", "a"), axis=0, tiled=True)

    steps, chunks = [0], [early, late]
    up, down = [early, late], [early, late]
    for step in range(1, N // 2):
        up = [send(part, shift_y(1)) for part in up]
        down = [send(part, shift_y(-1)) for part in down]
        steps += [step, -step]
        chunks += up + down
    steps.append(N // 2)
    chunks += [send(up[0], shift_y(1)), send(down[1], shift_y(-1))]

    given = send(gram_tile(False, pair_live, rows, steps, chunks), swap_lag())
    kept = gram_tile(True, pair_live, rows, steps, chunks)
    return lax.dynamic_update_slice(kept, given, (0, (1 - col_half(z, xh)) * HALF))


def solution(mesh):
    fine = Mesh(mesh.devices.reshape(N, 2, N, 2, 2), AX)
    return jax.shard_map(
        on_device,
        mesh=fine,
        in_specs=(P(("y", "xl", "z", "a"), "xh"), P()),
        out_specs=P(("y", "xl", "xh"), ("z", "a")),
        check_vma=False,
    )
```
